256 devices in a mesh: dp: 4 (over x_lo, core), seq: 32 (over z, y), mp: 2 (over x_hi).
Axes of the slice: x: 4 (x_hi: 2, x_lo: 2; x = x_hi * 2 + x_lo), y: 4, z: 8, core: 2. Of those that a mesh axis runs over, the one named last changes fastest.
Arguments:
- queries: bfloat16 [4, 4096, 2048], P('dp', 'seq', 'mp'), may hold values from -6 to 6
- keys: bfloat16 [4, 4096, 2048], P('dp', 'seq', 'mp'), may hold values from -6 to 6
- values: bfloat16 [4, 4096, 2048], P('dp', 'seq', 'mp'), may hold values from -6 to 6
- cross_queries: bfloat16 [4, 4096, 2048], P('dp', 'seq', 'mp'), may hold values from -6 to 6
- neighbour_ids: int32 [4, 64, 2, 2], P('dp', 'seq'), may hold values from 0 to 5, as said below
- database: bfloat16 [4, 2, 6, 128, 2048], P('dp', None, None, None, 'mp'), may hold values from -6 to 6
- out_weight: bfloat16 [2048, 4096], P('mp'), may hold values from -2.5 to 2.5
Outputs:
- mixed: bfloat16 [4, 4096, 4096], P('dp', 'seq', 'mp')
The draws below stay inside these ranges and needn't reach their ends.
Inputs may be any that keep to these rules, and one draw needn't show every extreme that they name: `neighbour_ids`: entry [b, c, n, 0] is the database shard and [b, c, n, 1] the block of the n-th neighbour of span c of sequence b. Among the neighbours of the 2 spans held by one index of dp and seq, at most 3 name one shard; in every draw, for some seq index, the spans of every dp index name exactly 3 neighbours of one common shard.
All inputs are finite; a program needn't handle non-finite values.
Results may differ from the reference program's by a relative error of at most 0.012.
Values may be sent and summed in bfloat16 or wider, within the bound.
No kernel may reach another device: no remote copies, remote signals or barrier semaphores. Data moves between devices by JAX's collectives and lax.ppermute only.
A program may use at most 128 MiB of HBM per device.

```python
import math
import jax
import jax.numpy as jnp
from jax import lax

D = 4096
HD = 128
SPAN = 64
NEIGH = 2
RETR = 128
HEADS = 16
TOK_DEV = 128
DB_BLOCKS = 6
FEAT = 2048
LENGTH = 4096
SPANS = 64
BATCH = 4
SHARDS = 4
CAP = 3


def neighbour_table(key):
    base = jax.random.fold_in(key, 7001)
    splits = jax.random.split(base, 7)
    spans_here = TOK_DEV // SPAN
    per_device = spans_here * NEIGH
    groups = SPANS // spans_here
    hottest = jax.random.randint(splits[0], (groups,), 0, SHARDS)
    flagged = jax.random.randint(splits[1], (BATCH, groups), 0, 2)
    forced = jax.random.randint(splits[2], (), 0, groups)
    flagged = jnp.where(jnp.arange(groups)[None, :] == forced, 1, flagged)
    rank_list = jnp.arange(per_device)
    hot_wide = hottest[None, :, None]
    others = (hot_wide + 1 + jax.random.randint(splits[3], (BATCH, groups, per_device), 0, SHARDS - 1)) % SHARDS
    shifts = jax.random.randint(splits[4], (BATCH, groups, 1), 0, SHARDS - 1)
    cycled = (hot_wide + 1 + (rank_list[None, None, :] + shifts) % (SHARDS - 1)) % SHARDS
    hot_heavy = jnp.where(rank_list[None, None, :] < CAP, hot_wide, others)
    shard_ids = jnp.where(flagged[:, :, None] == 1, hot_heavy, cycled)
    shuffle_keys = jax.random.randint(splits[5], (BATCH, groups, per_device), 0, 1 << 20) * per_device + rank_list[None, None, :]
    ordering = jnp.argsort(shuffle_keys, axis=-1, stable=True)
    shard_ids = jnp.take_along_axis(shard_ids, ordering, axis=-1)
    block_ids = jax.random.randint(splits[6], (BATCH, groups, per_device), 0, DB_BLOCKS)
    id_table = jnp.stack([shard_ids, block_ids], axis=-1)
    return id_table.reshape(BATCH, SPANS, NEIGH, 2).astype(jnp.int32)


def self_pair(key):
    base = jax.random.fold_in(key, 7005)
    first_key, second_key = jax.random.split(base, 2)
    query_draw = jnp.clip(jax.random.normal(first_key, (BATCH, LENGTH, FEAT), jnp.float32) * 1.3, -6.0, 6.0)
    key_draw = jnp.clip(jax.random.normal(second_key, (BATCH, LENGTH, FEAT), jnp.float32) * 1.3, -6.0, 6.0)
    return (query_draw, key_draw)


def draw_queries(key, part):
    return self_pair(key)[0].astype(jnp.bfloat16)


def draw_keys(key, part):
    return self_pair(key)[1].astype(jnp.bfloat16)


def draw_neighbour_ids(key, part):
    return neighbour_table(key)


def draw_cross_queries(key, part):
    base = jax.random.fold_in(key, 7003)
    cross_draw = jnp.clip(jax.random.normal(base, (BATCH, LENGTH, FEAT), jnp.float32) * 1.3, -6.0, 6.0)
    return cross_draw.astype(jnp.bfloat16)


def draw_database(key, part):
    base = jax.random.fold_in(key, 7002)
    first_key, second_key = jax.random.split(base, 2)
    key_part = jnp.clip(jax.random.normal(first_key, (SHARDS, DB_BLOCKS, RETR, FEAT), jnp.float32) * 1.3, -6.0, 6.0)
    value_part = jnp.clip(jax.random.normal(second_key, (SHARDS, DB_BLOCKS, RETR, FEAT), jnp.float32), -6.0, 6.0)
    return jnp.stack([key_part, value_part], axis=1).astype(jnp.bfloat16)


def levels(key, dims, pieces, least, top_value):
    level = 1.0
    for dim, shards_of in pieces:
        draws = jax.random.uniform(jax.random.fold_in(jax.random.fold_in(key, 6), dim), (shards_of,), jnp.float32, least / len(pieces), top_value / len(pieces))
        level = level * jnp.repeat(jnp.exp(draws), dims[dim] // shards_of).reshape((-1,) + (1,) * (len(dims) - 1 - dim))
    return level


def bell_draw(rng, extent, deviation, bound, cuts=(), kind=jnp.bfloat16):
    entries = jax.random.normal(rng, extent, jnp.float32) * deviation
    if len(cuts) > 0:
        entries = levels(rng, extent, cuts, -0.22, 0.18) * entries
    return jnp.clip(entries, min=-bound, max=bound).astype(kind)


def setup_inputs(seed: int = 0) -> dict:
    streams_of = jax.random.split(jax.random.key(seed), 8)
    queries = draw_queries(jax.random.fold_in(streams_of[7], 71), 0)
    keys = draw_keys(jax.random.fold_in(streams_of[7], 71), 0)
    values = bell_draw(streams_of[2], (BATCH, LENGTH, FEAT), 1.0, 6.0, ((0, 4), (1, 32), (2, 2)))
    cross_queries = draw_cross_queries(jax.random.fold_in(streams_of[7], 71), 0)
    neighbour_ids = draw_neighbour_ids(jax.random.fold_in(streams_of[7], 71), 0)
    database = draw_database(jax.random.fold_in(streams_of[7], 71), 0)
    out_weight = bell_draw(streams_of[6], (FEAT, D), 0.2, 2.5, ((0, 2),))
    return dict(queries=queries, keys=keys, values=values, cross_queries=cross_queries, neighbour_ids=neighbour_ids, database=database, out_weight=out_weight)


masked_score = -1e+30

def self_attend(query_seq, key_seq, value_seq):
    score_scale = 1.0 / math.sqrt(HD)
    key_heads = key_seq.reshape(LENGTH, HEADS, HD).astype(jnp.float32)
    value_heads = value_seq.reshape(LENGTH, HEADS, HD).astype(jnp.float32)
    query_blocks = query_seq.reshape(LENGTH // TOK_DEV, TOK_DEV, HEADS, HD)
    block_starts = (jnp.arange(LENGTH // TOK_DEV) * TOK_DEV).astype(jnp.int32)
    key_pos = jnp.arange(LENGTH).astype(jnp.int32)

    def one_block(operands):
        block_rows, block_start = operands
        scores = jnp.einsum('qhe,khe->hqk', block_rows.astype(jnp.float32), key_heads) * score_scale
        query_pos = block_start + jnp.arange(TOK_DEV).astype(jnp.int32)
        allowed = (key_pos[None, :] <= query_pos[:, None])[None]
        scores = jnp.where(allowed, scores, masked_score)
        row_max = lax.optimization_barrier(jnp.max(scores, axis=2, keepdims=True))
        weights = jnp.where(allowed, jnp.exp(scores - row_max), 0.0)
        totals = lax.optimization_barrier(jnp.sum(weights, axis=2))
        rounded = lax.optimization_barrier(weights.astype(jnp.bfloat16)).astype(jnp.float32)
        summed = jnp.einsum('hqk,khe->qhe', rounded, value_heads)
        return (summed / jnp.transpose(totals)[:, :, None]).reshape(TOK_DEV, HEADS * HD)
    return lax.map(one_block, (query_blocks, block_starts)).reshape(LENGTH, HEADS * HD)

def cross_attend(cross_seq, id_seq, database):
    score_scale = 1.0 / math.sqrt(HD)
    padded = jnp.concatenate([jnp.zeros((1, FEAT), cross_seq.dtype), cross_seq, jnp.zeros((SPAN - 1, FEAT), cross_seq.dtype)], axis=0)
    padded = padded.reshape(SPANS + 1, SPAN, HEADS, HD)

    def one_group(operands):
        group_rows, group_index = operands
        source = jnp.maximum(group_index - 1, 0)
        chosen = id_seq[source]
        picked_keys = database[chosen[:, 0], 0, chosen[:, 1]].reshape(NEIGH * RETR, HEADS, HD).astype(jnp.float32)
        picked_values = database[chosen[:, 0], 1, chosen[:, 1]].reshape(NEIGH * RETR, HEADS, HD).astype(jnp.float32)
        scores = jnp.einsum('qhe,khe->hqk', group_rows.astype(jnp.float32), picked_keys) * score_scale
        row_max = lax.optimization_barrier(jnp.max(scores, axis=2, keepdims=True))
        weights = jnp.exp(scores - row_max)
        totals = lax.optimization_barrier(jnp.sum(weights, axis=2))
        rounded = lax.optimization_barrier(weights.astype(jnp.bfloat16)).astype(jnp.float32)
        summed = jnp.einsum('hqk,khe->qhe', rounded, picked_values)
        live = (group_index >= 1).astype(jnp.float32)
        return (summed / jnp.transpose(totals)[:, :, None]).reshape(SPAN, FEAT) * live
    group_ids = jnp.arange(SPANS + 1).astype(jnp.int32)
    outputs = lax.map(one_group, (padded, group_ids))
    return outputs.reshape((SPANS + 1) * SPAN, FEAT)[1:1 + LENGTH]

def reference(queries, keys, values, cross_queries, neighbour_ids, database, out_weight):
    results = []
    for batch_index in range(BATCH):
        self_out = self_attend(queries[batch_index], keys[batch_index], values[batch_index])
        cross_out = cross_attend(cross_queries[batch_index], neighbour_ids[batch_index], database)
        attended = (self_out + cross_out).astype(jnp.bfloat16)
        results.append(jnp.dot(attended, out_weight, preferred_element_type=jnp.float32).astype(jnp.bfloat16))
    return jnp.stack(results)
```

```python
import functools
import math

import jax
import jax.numpy as jnp
from jax import lax
from jax.experimental import pallas as pl
from jax.experimental.pallas import tpu as pltpu
from jax.sharding import Mesh, PartitionSpec as P

HD = 128
ROWS = 128
HEADS = 8
ZS, YS = 8, 4
RETR = 128
STAT = 32
LOW = -1e30
EXP2_SCALE = math.log2(math.e) / math.sqrt(HD)
VMEM_LIMIT = 56 * 1024 * 1024

VMEM = pl.BlockSpec(memory_space=pltpu.VMEM)
SMEM = pl.BlockSpec(memory_space=pltpu.SMEM)
F32 = jnp.float32
BF16 = jnp.bfloat16


def params():
    return pltpu.CompilerParams(vmem_limit_bytes=VMEM_LIMIT)


def flipped(block):
    return jnp.transpose(block.astype(F32)).astype(BF16)


def split_kernel(q_ref, k_ref, v_ref, qt_ref, k_out, vt_ref):
    for h in range(HEADS):
        cols = pl.ds(h * HD, HD)
        k_out[h] = k_ref[:, cols]
        qt_ref[h] = flipped(q_ref[:, cols])
        vt_ref[h] = flipped(v_ref[:, cols])


def split_heads(queries, keys, values):
    shape = jax.ShapeDtypeStruct((HEADS, ROWS, HD), BF16)
    return pl.pallas_call(
        split_kernel,
        out_shape=(shape, shape, shape),
        in_specs=[VMEM] * 3,
        out_specs=(VMEM,) * 3,
        compiler_params=params(),
        name="split_heads",
        cost_estimate=pl.CostEstimate(flops=0, bytes_accessed=1536 * 1024, transcendentals=0),
    )(queries, keys, values)


PART_STEPS = (0, YS - 1, 1, 2)


def self_kernel(y_ref, qt_ref, *refs):
    k_refs, v_refs, out_ref, bias, wide = refs[0:4], refs[4:8], refs[8], refs[9], refs[10]
    y = y_ref[0]
    tile = len(k_refs) * ROWS
    key_pos = lax.broadcasted_iota(jnp.int32, (ROWS, ROWS), 0)
    query_pos = lax.broadcasted_iota(jnp.int32, (ROWS, ROWS), 1)
    bias[0:ROWS, :] = jnp.where(key_pos <= query_pos, 0.0, LOW)
    for part in range(1, 4):
        earlier = lax.rem(y + PART_STEPS[part], YS) < y
        shade = jnp.where(earlier, 0.0, LOW).astype(F32)
        bias[part * ROWS : (part + 1) * ROWS, :] = jnp.full((ROWS, ROWS), shade, F32)

    for pair in range(ZS // 2):
        wide[:, 0:ROWS] = qt_ref[2 * pair]
        wide[:, ROWS:] = qt_ref[2 * pair + 1]

        def visit(z, state, side, added):
            row_max, total, summed = state
            k_tile = jnp.concatenate([k[z] for k in k_refs], axis=0)
            v_tile = jnp.concatenate([v[z] for v in v_refs], axis=1)
            scores = jnp.dot(k_tile, wide[:, side], preferred_element_type=F32)
            if added is not None:
                scores = scores + added
            new_max = jnp.maximum(row_max, jnp.max(scores, axis=0, keepdims=True))
            weights = jnp.exp2((scores - new_max) * EXP2_SCALE)
            fade = jnp.exp2((row_max - new_max) * EXP2_SCALE)
            total = total * fade + jnp.sum(weights, axis=0, keepdims=True)
            summed = summed * fade + jnp.dot(
                v_tile, weights.astype(BF16), preferred_element_type=F32
            )
            return new_max, total, summed

        width = 2 * ROWS
        state = (
            jnp.full((1, width), LOW, F32),
            jnp.zeros((1, width), F32),
            jnp.zeros((HD, width), F32),
        )
        shade = bias[...]
        clear = jnp.zeros((tile, ROWS), F32)
        state = visit(2 * pair, state, slice(None), jnp.concatenate([shade, clear], axis=1))
        for z in range(2 * pair):
            state = visit(z, state, slice(None), None)
        left = [part[:, :ROWS] for part in state]
        right = [part[:, ROWS:] for part in state]
        right = visit(2 * pair + 1, right, slice(ROWS, None), shade)
        out_ref[2 * pair] = (left[2] / left[1]).astype(BF16)
        out_ref[2 * pair + 1] = (right[2] / right[1]).astype(BF16)


def self_attend(y_index, qt, key_parts, value_parts):
    return pl.pallas_call(
        self_kernel,
        out_shape=jax.ShapeDtypeStruct((ZS, HD, ROWS), BF16),
        in_specs=[SMEM] + [VMEM] * 9,
        out_specs=VMEM,
        scratch_shapes=[pltpu.VMEM((4 * ROWS, ROWS), F32), pltpu.VMEM((HD, 2 * ROWS), BF16)],
        compiler_params=params(),
        name="self_attend",
        cost_estimate=pl.CostEstimate(
            flops=1_300_000_000, bytes_accessed=2_500_000, transcendentals=2_600_000
        ),
    )(y_index, qt, *key_parts, *value_parts)


def cross_kernel(ids_ref, place_ref, *refs):
    q_refs, db_ref, out_refs = refs[0:4], refs[4], refs[5:9]
    top, total, summed = refs[9:12]
    here = place_ref[0]
    row = lax.broadcasted_iota(jnp.int32, (1, ROWS), 1)
    group_of = (row + 1) // 64
    for away in range(4):
        home = (
            lax.rem(here // 2 + away // 2, 2) * 2 + lax.rem(lax.rem(here, 2) + away % 2, 2)
        )
        top[...] = jnp.full(top.shape, LOW, F32)
        total[...] = jnp.zeros(total.shape, F32)
        summed[...] = jnp.zeros(summed.shape, F32)

        def neighbour(index, carry, away=away, home=home):
            shard = ids_ref[home, 2 * index]
            block = ids_ref[home, 2 * index + 1]

            @pl.when(shard == here)
            def _():
                inside = group_of == index // 2
                for h in range(HEADS):
                    cols = pl.ds(h * HD, HD)
                    key_rows = db_ref[0, block, :, cols]
                    value_rows = db_ref[1, block, :, cols]
                    scores = lax.dot_general(
                        key_rows,
                        q_refs[away][:, cols],
                        (((1,), (1,)), ((), ())),
                        preferred_element_type=F32,
                    )
                    old_max = top[h : h + 1, :]
                    new_max = jnp.maximum(old_max, jnp.max(scores, axis=0, keepdims=True))
                    new_max = jnp.where(inside, new_max, old_max)
                    weights = jnp.where(inside, jnp.exp2((scores - new_max) * EXP2_SCALE), 0.0)
                    fade = jnp.exp2((old_max - new_max) * EXP2_SCALE)
                    top[h : h + 1, :] = new_max
                    total[h : h + 1, :] = total[h : h + 1, :] * fade + jnp.sum(
                        weights, axis=0, keepdims=True
                    )
                    summed[cols, :] = summed[cols, :] * fade + lax.dot_general(
                        value_rows,
                        weights.astype(BF16),
                        (((0,), (0,)), ((), ())),
                        preferred_element_type=F32,
                    )

            return carry

        lax.fori_loop(0, 6, neighbour, 0)
        out_ref = out_refs[away]
        sums = total[...]
        some = sums > 0.0
        safe = jnp.where(some, sums, 1.0)
        for h in range(HEADS):
            cols = pl.ds(h * HD, HD)
            out_ref[cols, :] = (summed[cols, :] / safe[h : h + 1, :]).astype(BF16)
        level = jnp.where(some, top[...] * EXP2_SCALE + jnp.log2(safe), LOW)
        high = level.astype(BF16).astype(F32)
        middle = (level - high).astype(BF16).astype(F32)
        low = level - high - middle
        stats = jnp.concatenate([high, middle, low, jnp.zeros_like(low)], axis=0)
        out_ref[HEADS * HD :, :] = stats.astype(BF16)


def cross_attend(ids, place, queries_by_distance, database):
    shape = jax.ShapeDtypeStruct((HEADS * HD + STAT, ROWS), BF16)
    return pl.pallas_call(
        cross_kernel,
        out_shape=(shape,) * 4,
        in_specs=[SMEM, SMEM] + [VMEM] * 5,
        out_specs=(VMEM,) * 4,
        scratch_shapes=[
            pltpu.VMEM((HEADS, ROWS), F32),
            pltpu.VMEM((HEADS, ROWS), F32),
            pltpu.VMEM((HEADS * HD, ROWS), F32),
        ],
        compiler_params=params(),
        name="cross_attend",
        cost_estimate=pl.CostEstimate(
            flops=1_000_000_000, bytes_accessed=5_500_000, transcendentals=1_000_000
        ),
    )(ids, place, *queries_by_distance, database)


COLS = 2048
TILE = 512


def join_kernel(place_ref, self_ref, *refs):
    part_refs, w_ref, att_ref, out_ref = refs[0:4], refs[4], refs[5], refs[6]

    @pl.when(pl.program_id(0) == 0)
    def _():
        row = lax.broadcasted_iota(jnp.int32, (1, ROWS), 1)
        live = jnp.where((row >= 63) | (place_ref[1] > 0), 1.0, 0.0).astype(F32)
        levels = []
        for part in part_refs:
            stats = part[HEADS * HD :, :].astype(F32)
            levels.append(stats[0:8] + stats[8:16] + stats[16:24])
        top = functools.reduce(jnp.maximum, levels)
        shares = [jnp.exp2(level - top) for level in levels]
        whole = functools.reduce(jnp.add, shares)
        shares = [share / whole * live for share in shares]
        for h in range(HEADS):
            cols = pl.ds(h * HD, HD)
            joined = self_ref[h].astype(F32)
            for part, share in zip(part_refs, shares):
                joined = joined + part[cols, :].astype(F32) * share[h : h + 1, :]
            att_ref[:, cols] = jnp.transpose(joined).astype(BF16)

    out_ref[...] = jnp.dot(att_ref[...], w_ref[...], preferred_element_type=F32).astype(BF16)


def join_and_project(place, self_parts, cross_parts, out_weight):
    tiles = COLS // TILE
    fixed2 = lambda shape: pl.BlockSpec(shape, lambda i, place: (0,) * len(shape))
    return pl.pallas_call(
        join_kernel,
        out_shape=(
            jax.ShapeDtypeStruct((ROWS, HEADS * HD), BF16),
            jax.ShapeDtypeStruct((ROWS, COLS), BF16),
        ),
        grid_spec=pltpu.PrefetchScalarGridSpec(
            num_scalar_prefetch=1,
            grid=(tiles,),
            in_specs=[fixed2((HEADS, HD, ROWS))]
            + [fixed2((HEADS * HD + STAT, ROWS))] * 4
            + [
                pl.BlockSpec(
                    (HEADS * HD, TILE), lambda i, place: (0, (1 - place[0]) * tiles + i)
                )
            ],
            out_specs=(
                fixed2((ROWS, HEADS * HD)),
                pl.BlockSpec((ROWS, TILE), lambda i, place: (0, i)),
            ),
        ),
        compiler_params=params(),
        name="join_and_project",
        cost_estimate=pl.CostEstimate(
            flops=540_000_000, bytes_accessed=6_000_000, transcendentals=4096
        ),
    )(place, self_parts, *cross_parts, out_weight)


def project_kernel(place_ref, att_ref, w_ref, out_ref):
    out_ref[...] = jnp.dot(att_ref[...], w_ref[...], preferred_element_type=F32).astype(BF16)


def project_own(place, attended, out_weight):
    tiles = COLS // TILE
    return pl.pallas_call(
        project_kernel,
        out_shape=jax.ShapeDtypeStruct((ROWS, COLS), BF16),
        grid_spec=pltpu.PrefetchScalarGridSpec(
            num_scalar_prefetch=1,
            grid=(tiles,),
            in_specs=[
                pl.BlockSpec((ROWS, HEADS * HD), lambda i, place: (0, 0)),
                pl.BlockSpec((HEADS * HD, TILE), lambda i, place: (0, place[0] * tiles + i)),
            ],
            out_specs=pl.BlockSpec((ROWS, TILE), lambda i, place: (0, i)),
        ),
        compiler_params=params(),
        name="project_own",
        cost_estimate=pl.CostEstimate(
            flops=540_000_000, bytes_accessed=5_000_000, transcendentals=0
        ),
    )(place, attended, out_weight)


def ring(axis, step):
    count = lax.axis_size(axis)
    return [(i, (i + step) % count) for i in range(count)]


def per_device(queries, keys, values, cross_queries, neighbour_ids, database, out_weight):
    dp = ("xl", "core")
    seq = ("z", "y")
    seq_index = lax.axis_index(seq)
    y_index = lax.axis_index("y").astype(jnp.int32).reshape(1)
    place_dp = lax.axis_index(dp).astype(jnp.int32).reshape(1)
    place = jnp.stack([lax.axis_index("xh"), seq_index]).astype(jnp.int32)
    across, beside = ring("xl", 1), ring("core", 1)

    mine = cross_queries[0]
    from_across = lax.ppermute(mine, "xl", across)
    from_beside = lax.ppermute(mine, "core", beside)
    from_diagonal = lax.ppermute(from_across, "core", beside)
    own_ids = neighbour_ids[0].reshape(2, 4)
    earlier_ids = lax.ppermute(own_ids[1:], seq, [(i, i + 1) for i in range(ZS * YS - 1)])
    ids = jnp.concatenate([earlier_ids, own_ids], axis=0).reshape(1, 12)
    ids = lax.all_gather(ids, dp, axis=0, tiled=True)

    qt, k, vt = split_heads(queries[0], keys[0], values[0])
    k = lax.all_to_all(k, "z", 0, 0, tiled=True)
    vt = lax.all_to_all(vt, "z", 0, 0, tiled=True)
    qt = lax.all_to_all(qt, "z", 0, 0, tiled=True)
    up, down = ring("y", 1), ring("y", -1)
    k_below, v_below = (lax.ppermute(a, "y", up) for a in (k, vt))
    k_above, v_above = (lax.ppermute(a, "y", down) for a in (k, vt))
    k_far = lax.ppermute(k_below, "y", up)
    v_far = lax.ppermute(v_above, "y", down)

    parts = cross_attend(
        ids, place_dp, (mine, from_beside, from_across, from_diagonal), database[0]
    )
    own_part = parts[0]
    beside_part = lax.ppermute(parts[1], "core", beside)
    across_part = lax.ppermute(parts[2], "xl", across)
    diagonal_part = lax.ppermute(parts[3], dp, [(i, 3 - i) for i in range(4)])

    self_t = self_attend(
        y_index, qt, (k, k_below, k_above, k_far), (vt, v_below, v_above, v_far)
    )
    self_t = lax.all_to_all(self_t, "z", 0, 0, tiled=True)

    attended, theirs = join_and_project(
        place, self_t, (own_part, beside_part, across_part, diagonal_part), out_weight
    )
    received = lax.ppermute(theirs, "xh", ring("xh", 1))
    kept = project_own(place, attended, out_weight)
    return (kept.astype(F32) + received.astype(F32)).astype(BF16)[None]


def solution(mesh):
    split = Mesh(mesh.devices.reshape(2, 2, ZS, YS, 2), ("xl", "core", "z", "y", "xh"))
    dp, seq = ("xl", "core"), ("z", "y")
    placed = (
        P(dp, seq, "xh"),
        P(dp, seq, "xh"),
        P(dp, seq, "xh"),
        P(dp, seq, "xh"),
        P(dp, seq, None, None),
        P(dp, None, None, None, "xh"),
        P("xh", None),
    )
    return jax.shard_map(
        per_device, mesh=split, in_specs=placed, out_specs=P(dp, seq, "xh"), check_vma=False
    )
```

```python
import functools
import math

import jax
import jax.numpy as jnp
from jax import lax
from jax.experimental import pallas as pl
from jax.experimental.pallas import tpu as pltpu
from jax.sharding import Mesh, PartitionSpec as P

HD = 128
ROWS = 128
HEADS = 8
ZS, YS = 8, 4
RETR = 128
STAT = 32
LOW = -1e30
EXP2_SCALE = math.log2(math.e) / math.sqrt(HD)
VMEM_LIMIT = 24 * 1024 * 1024

VMEM = pl.BlockSpec(memory_space=pltpu.VMEM)
SMEM = pl.BlockSpec(memory_space=pltpu.SMEM)
F32 = jnp.float32
BF16 = jnp.bfloat16


def params(limit=VMEM_LIMIT):
    return pltpu.CompilerParams(vmem_limit_bytes=limit)


def flipped(block):
    return jnp.transpose(block.astype(F32)).astype(BF16)


def split_kernel(q_ref, k_ref, v_ref, out_ref):
    for h in range(HEADS):
        cols = pl.ds(h * HD, HD)
        out_ref[h, 0] = k_ref[:, cols]
        out_ref[h, 1] = flipped(v_ref[:, cols])
        out_ref[h, 2] = flipped(q_ref[:, cols])


def split_heads(queries, keys, values):
    return pl.pallas_call(
        split_kernel,
        out_shape=jax.ShapeDtypeStruct((HEADS, 3, ROWS, HD), BF16),
        in_specs=[VMEM] * 3,
        out_specs=VMEM,
        compiler_params=params(56 * 1024 * 1024),
        name="split_heads",
        cost_estimate=pl.CostEstimate(flops=0, bytes_accessed=1536 * 1024, transcendentals=0),
    )(queries, keys, values)


def shade_of(y, step):
    return jnp.where(lax.rem(y + step, YS) < y, 0.0, LOW).astype(F32)


def fold(state, scores, v_tile):
    row_max, total, summed = state
    new_max = jnp.maximum(row_max, jnp.max(scores, axis=0, keepdims=True))
    weights = jnp.exp2((scores - new_max) * EXP2_SCALE)
    fade = jnp.exp2((row_max - new_max) * EXP2_SCALE)
    total = total * fade + jnp.sum(weights, axis=0, keepdims=True)
    summed = summed * fade + jnp.dot(v_tile, weights.astype(BF16), preferred_element_type=F32)
    return new_max, total, summed


def attend_kernel(steps, count, first, last, y_ref, own_ref, *refs):
    part_refs, refs = refs[:count], refs[count:]
    if not first:
        old_refs, refs = refs[:3], refs[3:]
    wide, results = refs[-1], refs[:-1]
    y = y_ref[0]
    left = lax.broadcasted_iota(jnp.int32, (1, 2 * ROWS), 1) < ROWS
    key_pos = lax.broadcasted_iota(jnp.int32, (ROWS, 2 * ROWS), 0)
    query_pos = lax.broadcasted_iota(jnp.int32, (ROWS, 2 * ROWS), 1)
    halves = count // len(steps)

    def block(part, z, kind):
        depth = ZS // halves
        return part_refs[part * halves + z // depth][z % depth, kind]

    for pair in range(ZS // 2):
        low, high = 2 * pair, 2 * pair + 1
        wide[:, 0:ROWS] = own_ref[low, 2]
        wide[:, ROWS:] = own_ref[high, 2]
        places = [(part, z) for part in range(len(steps)) for z in range(high + 1)]
        k_tile = jnp.concatenate([block(part, z, 0) for part, z in places], axis=0)
        v_tile = jnp.concatenate([block(part, z, 1) for part, z in places], axis=1)
        scores = jnp.dot(k_tile, wide[...], preferred_element_type=F32)
        pieces = []
        for part, step in enumerate(steps):
            start = part * (high + 1) * ROWS
            middle, end = start + low * ROWS, start + high * ROWS
            if step == 0:
                same_z = jnp.where(left & (key_pos > query_pos), LOW, 0.0)
                next_z = jnp.where(left | (key_pos > query_pos - ROWS), LOW, 0.0)
            else:
                shade = shade_of(y, step)
                same_z, next_z = jnp.where(left, shade, 0.0), jnp.where(left, LOW, shade)
            if low:
                pieces.append(scores[start:middle])
            pieces.append(scores[middle:end] + same_z)
            pieces.append(scores[end : end + ROWS] + next_z)
        scores = jnp.concatenate(pieces, axis=0)
        if first:
            row_max = jnp.max(scores, axis=0, keepdims=True)
            weights = jnp.exp2((scores - row_max) * EXP2_SCALE)
            total = jnp.sum(weights, axis=0, keepdims=True)
            summed = jnp.dot(v_tile, weights.astype(BF16), preferred_element_type=F32)
        else:
            old = [
                jnp.concatenate([ref[z : z + 1, :] for z in (low, high)], axis=1)
                for ref in old_refs[:2]
            ] + [jnp.concatenate([old_refs[2][z] for z in (low, high)], axis=1)]
            row_max, total, summed = fold(old, scores, v_tile)
        for z, side in ((low, slice(0, ROWS)), (high, slice(ROWS, None))):
            if last:
                results[0][z] = (summed[:, side] * (1.0 / total[:, side])).astype(BF16)
            else:
                results[0][z : z + 1, :] = row_max[:, side]
                results[1][z : z + 1, :] = total[:, side]
                results[2][z] = summed[:, side]


def attend(y_index, own, steps, parts, state=(), last=False):
    rows = jax.ShapeDtypeStruct((ZS, ROWS), F32)
    kept = (rows, rows, jax.ShapeDtypeStruct((ZS, HD, ROWS), F32))
    share = len(steps)
    return pl.pallas_call(
        functools.partial(attend_kernel, steps, len(parts), not state, last),
        out_shape=jax.ShapeDtypeStruct((ZS, HD, ROWS), BF16) if last else kept,
        in_specs=[SMEM] + [VMEM] * (1 + len(parts) + len(state)),
        out_specs=VMEM if last else (VMEM,) * 3,
        scratch_shapes=[pltpu.VMEM((HD, 2 * ROWS), BF16)],
        compiler_params=params(),
        name="attend_far" if last else "attend_near",
        cost_estimate=pl.CostEstimate(
            flops=350_000_000 * share, bytes_accessed=1_500_000, transcendentals=650_000 * share
        ),
    )(y_index, own, *parts, *state)


def cross_kernel(ids0_ref, ids1_ref, place_ref, q0_ref, q1_ref, db_ref, out0_ref, out1_ref, *refs):
    top, total, summed, blocks, queries, arrived, ready = refs
    here = place_ref[0]
    fetches = [
        pltpu.make_async_copy(q_ref, queries.at[slot], arrived.at[slot])
        for slot, q_ref in enumerate((q0_ref, q1_ref))
    ]
    for fetch in fetches:
        fetch.start()

    def named(ids_ref, index):
        which, span, n = (index + 2) // 4, lax.rem(index // 2 + 1, 2), lax.rem(index, 2)
        return ids_ref[which, span, n, 0], ids_ref[which, span, n, 1]

    def fetch_block(block, place):
        return pltpu.make_async_copy(db_ref.at[:, block], blocks.at[place], ready.at[place])

    for slot, ids_ref in enumerate((ids0_ref, ids1_ref)):

        def request(index, carry, slot=slot, ids_ref=ids_ref):
            shard, block = named(ids_ref, index)

            @pl.when(shard == here)
            def _():
                fetch_block(block, 6 * slot + index).start()

            return carry

        lax.fori_loop(0, 6, request, 0)
    for fetch in fetches:
        fetch.wait()
    row = lax.broadcasted_iota(jnp.int32, (1, ROWS), 1)
    group_of = (row + 1) // 64
    for slot, ids_ref, out_ref in ((0, ids0_ref, out0_ref), (1, ids1_ref, out1_ref)):
        top[...] = jnp.full(top.shape, LOW, F32)
        total[...] = jnp.zeros(total.shape, F32)
        summed[...] = jnp.zeros(summed.shape, F32)

        def neighbour(index, carry, ids_ref=ids_ref, slot=slot):
            shard, block = named(ids_ref, index)
            place = 6 * slot + index

            @pl.when(shard == here)
            def _():
                fetch_block(block, place).wait()
                inside = group_of == index // 2
                cols = [slice(h * HD, (h + 1) * HD) for h in range(HEADS)]
                scores = [
                    lax.dot_general(
                        blocks[place, 0, :, c],
                        queries[slot, :, c],
                        (((1,), (1,)), ((), ())),
                        preferred_element_type=F32,
                    )
                    for c in cols
                ]
                old_max = top[...]
                new_max = jnp.concatenate(
                    [jnp.max(block_scores, axis=0, keepdims=True) for block_scores in scores], axis=0
                )
                new_max = jnp.where(inside, jnp.maximum(old_max, new_max), old_max)
                fade = jnp.exp2((old_max - new_max) * EXP2_SCALE)
                weights = [
                    jnp.where(
                        inside, jnp.exp2((scores[h] - new_max[h : h + 1]) * EXP2_SCALE), 0.0
                    )
                    for h in range(HEADS)
                ]
                sums = [jnp.sum(w, axis=0, keepdims=True) for w in weights]
                products = [
                    lax.dot_general(
                        blocks[place, 1, :, cols[h]],
                        weights[h].astype(BF16),
                        (((0,), (0,)), ((), ())),
                        preferred_element_type=F32,
                    )
                    for h in range(HEADS)
                ]
                top[...] = new_max
                total[...] = total[...] * fade + jnp.concatenate(sums, axis=0)
                for h in range(HEADS):
                    summed[h] = summed[h] * fade[h : h + 1] + products[h]

            return carry

        lax.fori_loop(0, 6, neighbour, 0)
        sums = total[...]
        some = sums > 0.0
        safe = jnp.where(some, sums, 1.0)
        inverse = 1.0 / safe
        for h in range(HEADS):
            out_ref[h * HD : (h + 1) * HD, :] = (summed[h] * inverse[h : h + 1, :]).astype(BF16)
        level = jnp.where(some, top[...] * EXP2_SCALE + jnp.log2(safe), LOW)
        high = level.astype(BF16).astype(F32)
        middle = (level - high).astype(BF16).astype(F32)
        low = level - high - middle
        stats = jnp.concatenate([high, middle, low, jnp.zeros_like(low)], axis=0)
        out_ref[HEADS * HD :, :] = stats.astype(BF16)


def cross_attend(place, ids, queries, database):
    shape = jax.ShapeDtypeStruct((HEADS * HD + STAT, ROWS), BF16)
    return pl.pallas_call(
        cross_kernel,
        out_shape=(shape,) * 2,
        in_specs=[SMEM] * 3 + [pl.BlockSpec(memory_space=pl.ANY)] * 3,
        out_specs=(VMEM,) * 2,
        scratch_shapes=[
            pltpu.VMEM((HEADS, ROWS), F32),
            pltpu.VMEM((HEADS, ROWS), F32),
            pltpu.VMEM((HEADS, HD, ROWS), F32),
            pltpu.VMEM((12, 2, RETR, HEADS * HD), BF16),
            pltpu.VMEM((2, ROWS, HEADS * HD), BF16),
            pltpu.SemaphoreType.DMA((2,)),
            pltpu.SemaphoreType.DMA((12,)),
        ],
        compiler_params=params(56 * 1024 * 1024),
        name="cross_attend",
        cost_estimate=pl.CostEstimate(
            flops=2_000_000_000, bytes_accessed=5_000_000, transcendentals=1_000_000
        ),
    )(*ids, place, *queries, database)


COLS = 2048


def join_kernel(place_ref, self_ref, *refs):
    part_refs, att_ref = refs[0:4], refs[4]
    row = lax.broadcasted_iota(jnp.int32, (1, ROWS), 1)
    live = jnp.where((row >= 63) | (place_ref[0] > 0), 1.0, 0.0).astype(F32)
    levels = []
    for part in part_refs:
        stats = part[HEADS * HD :, :].astype(F32)
        levels.append(stats[0:8] + stats[8:16] + stats[16:24])
    top = functools.reduce(jnp.maximum, levels)
    shares = [jnp.exp2(level - top) for level in levels]
    whole = functools.reduce(jnp.add, shares)
    shares = [share / whole * live for share in shares]
    for h in range(HEADS):
        cols = slice(h * HD, (h + 1) * HD)
        joined = self_ref[h].astype(F32)
        for part, share in zip(part_refs, shares):
            joined = joined + part[cols, :].astype(F32) * share[h : h + 1, :]
        att_ref[:, cols] = jnp.transpose(joined).astype(BF16)


def join(place, self_parts, cross_parts):
    return pl.pallas_call(
        join_kernel,
        out_shape=jax.ShapeDtypeStruct((ROWS, HEADS * HD), BF16),
        in_specs=[SMEM] + [VMEM] * 5,
        out_specs=VMEM,
        compiler_params=params(),
        name="join",
        cost_estimate=pl.CostEstimate(flops=0, bytes_accessed=1_500_000, transcendentals=4096),
    )(place, self_parts, *cross_parts)


PIECES = 4


def add_kernel(kept_ref, received_ref, out_ref, buffer, done):
    wide = COLS // PIECES
    copies = []
    for piece in range(PIECES):
        cols = slice(piece * wide, (piece + 1) * wide)
        buffer[:, cols] = (kept_ref[:, cols].astype(F32) + received_ref[:, cols].astype(F32)).astype(
            BF16
        )
        copies.append(
            pltpu.make_async_copy(buffer.at[:, cols], out_ref.at[:, cols], done.at[piece])
        )
        copies[-1].start()
    for copy in copies:
        copy.wait()


def add(kept, received):
    return pl.pallas_call(
        add_kernel,
        out_shape=jax.ShapeDtypeStruct((ROWS, COLS), BF16),
        in_specs=[VMEM] * 2,
        out_specs=pl.BlockSpec(memory_space=pl.ANY),
        scratch_shapes=[pltpu.VMEM((ROWS, COLS), BF16), pltpu.SemaphoreType.DMA((PIECES,))],
        compiler_params=params(),
        name="add",
        cost_estimate=pl.CostEstimate(flops=0, bytes_accessed=1_500_000, transcendentals=0),
    )(kept, received)


def ring(axis, step):
    count = lax.axis_size(axis)
    return [(i, (i + step) % count) for i in range(count)]


def per_device(queries, keys, values, cross_queries, neighbour_ids, database, out_weight):
    dp = ("xl", "core")
    seq = ("z", "y")
    seq_index = lax.axis_index(seq).astype(jnp.int32).reshape(1)
    y_index = lax.axis_index("y").astype(jnp.int32).reshape(1)
    place_dp = lax.axis_index(dp).astype(jnp.int32).reshape(1)
    across, beside = ring("xl", 1), ring("core", 1)
    up, down = ring("y", 1), ring("y", -1)

    earlier_ids = lax.ppermute(neighbour_ids, seq, [(i, i + 1) for i in range(ZS * YS - 1)])
    own = split_heads(queries[0], keys[0], values[0])
    own, earlier_ids = lax.optimization_barrier((own, earlier_ids))
    own = lax.all_to_all(own, "z", 0, 0, tiled=True)

    mine = cross_queries[0]
    ids = jnp.concatenate([earlier_ids, neighbour_ids], axis=0)
    from_across = lax.ppermute(mine, "xl", across)
    from_beside = lax.ppermute(mine, "core", beside)
    ids_across = lax.ppermute(ids, "xl", across)
    ids_beside = lax.ppermute(ids, "core", beside)
    own_part, beside_part = cross_attend(
        place_dp, (ids, ids_beside), (mine, from_beside), database[0]
    )
    from_across, ids_across, _ = lax.optimization_barrier((from_across, ids_across, own_part))
    from_diagonal = lax.ppermute(from_across, "core", beside)
    ids_diagonal = lax.ppermute(ids_across, "core", beside)
    across_part, diagonal_part = cross_attend(
        place_dp, (ids_across, ids_diagonal), (from_across, from_diagonal), database[0]
    )
    own, across_part, diagonal_part, beside_part = lax.optimization_barrier(
        (own, across_part, diagonal_part, beside_part)
    )

    kv = own[:, :2]
    below = lax.ppermute(kv, "y", up)
    above = lax.ppermute(kv, "y", down)
    beside_part = lax.ppermute(beside_part, "core", beside)
    across_part = lax.ppermute(across_part, "xl", across)
    diagonal_part = lax.ppermute(diagonal_part, dp, [(i, 3 - i) for i in range(4)])
    state = attend(y_index, own, (0,), (own,))
    below, above, state = lax.optimization_barrier((below, above, state))

    far_low = lax.ppermute(below[: ZS // 2], "y", up)
    far_high = lax.ppermute(above[ZS // 2 :], "y", down)
    state = attend(y_index, own, (YS - 1, 1), (below, above), state)
    far_low, far_high, state, beside_part, across_part, diagonal_part = lax.optimization_barrier(
        (far_low, far_high, state, beside_part, across_part, diagonal_part)
    )

    self_t = attend(y_index, own, (2,), (far_low, far_high), state, last=True)
    self_t = lax.all_to_all(self_t, "z", 0, 0, tiled=True)

    attended = join(seq_index, self_t, (own_part, beside_part, across_part, diagonal_part))
    xh = lax.axis_index("xh")

    def projected(half):
        columns = lax.dynamic_slice_in_dim(out_weight, half * COLS, COLS, axis=1)
        return jnp.dot(attended, columns, preferred_element_type=F32).astype(BF16)

    received = lax.ppermute(projected(1 - xh), "xh", ring("xh", 1))
    return add(projected(xh), received)[None]


def solution(mesh):
    split = Mesh(mesh.devices.reshape(2, 2, ZS, YS, 2), ("xl", "core", "z", "y", "xh"))
    dp, seq = ("xl", "core"), ("z", "y")
    placed = (
        P(dp, seq, "xh"),
        P(dp, seq, "xh"),
        P(dp, seq, "xh"),
        P(dp, seq, "xh"),
        P(dp, seq, None, None),
        P(dp, None, None, None, "xh"),
        P("xh", None),
    )
    return jax.shard_map(
        per_device, mesh=split, in_specs=placed, out_specs=P(dp, seq, "xh"), check_vma=False
    )
```

```python
import functools
import math

import jax
import jax.numpy as jnp
from jax import lax
from jax.experimental import pallas as pl
from jax.experimental.pallas import tpu as pltpu
from jax.sharding import Mesh, PartitionSpec as P

HD = 128
ROWS = 128
HEADS = 8
ZS, YS = 8, 4
RETR = 128
STAT = 32
LOW = -1e30
EXP2_SCALE = math.log2(math.e) / math.sqrt(HD)
VMEM_LIMIT = 24 * 1024 * 1024

VMEM = pl.BlockSpec(memory_space=pltpu.VMEM)
SMEM = pl.BlockSpec(memory_space=pltpu.SMEM)
F32 = jnp.float32
BF16 = jnp.bfloat16


def params(limit=VMEM_LIMIT):
    return pltpu.CompilerParams(vmem_limit_bytes=limit)


def flipped(block):
    return jnp.transpose(block.astype(F32)).astype(BF16)


def split_kernel(q_ref, k_ref, v_ref, out_ref):
    for h in range(HEADS):
        cols = pl.ds(h * HD, HD)
        out_ref[h, 0] = k_ref[:, cols]
        out_ref[h, 1] = flipped(v_ref[:, cols])
        out_ref[h, 2] = flipped(q_ref[:, cols])


def split_heads(queries, keys, values):
    return pl.pallas_call(
        split_kernel,
        out_shape=jax.ShapeDtypeStruct((HEADS, 3, ROWS, HD), BF16),
        in_specs=[VMEM] * 3,
        out_specs=VMEM,
        compiler_params=params(56 * 1024 * 1024),
        name="split_heads",
        cost_estimate=pl.CostEstimate(flops=0, bytes_accessed=1536 * 1024, transcendentals=0),
    )(queries, keys, values)


def shade_of(y, step):
    return jnp.where(lax.rem(y + step, YS) < y, 0.0, LOW).astype(F32)


def fold(state, scores, v_tile):
    row_max, total, summed = state
    new_max = jnp.maximum(row_max, jnp.max(scores, axis=0, keepdims=True))
    weights = jnp.exp2((scores - new_max) * EXP2_SCALE)
    fade = jnp.exp2((row_max - new_max) * EXP2_SCALE)
    total = total * fade + jnp.sum(weights, axis=0, keepdims=True)
    summed = summed * fade + jnp.dot(v_tile, weights.astype(BF16), preferred_element_type=F32)
    return new_max, total, summed


def attend_kernel(steps, count, first, last, y_ref, own_ref, *refs):
    part_refs, refs = refs[:count], refs[count:]
    if not first:
        old_refs, refs = refs[:3], refs[3:]
    wide, results = refs[-1], refs[:-1]
    y = y_ref[0]
    left = lax.broadcasted_iota(jnp.int32, (1, 2 * ROWS), 1) < ROWS
    key_pos = lax.broadcasted_iota(jnp.int32, (ROWS, 2 * ROWS), 0)
    query_pos = lax.broadcasted_iota(jnp.int32, (ROWS, 2 * ROWS), 1)
    halves = count // len(steps)

    def block(part, z, kind):
        depth = ZS // halves
        return part_refs[part * halves + z // depth][z % depth, kind]

    for pair in range(ZS // 2):
        low, high = 2 * pair, 2 * pair + 1
        wide[:, 0:ROWS] = own_ref[low, 2]
        wide[:, ROWS:] = own_ref[high, 2]
        places = [(part, z) for part in range(len(steps)) for z in range(high + 1)]
        k_tile = jnp.concatenate([block(part, z, 0) for part, z in places], axis=0)
        v_tile = jnp.concatenate([block(part, z, 1) for part, z in places], axis=1)
        scores = jnp.dot(k_tile, wide[...], preferred_element_type=F32)
        pieces = []
        for part, step in enumerate(steps):
            start = part * (high + 1) * ROWS
            middle, end = start + low * ROWS, start + high * ROWS
            if step == 0:
                same_z = jnp.where(left & (key_pos > query_pos), LOW, 0.0)
                next_z = jnp.where(left | (key_pos > query_pos - ROWS), LOW, 0.0)
            else:
                shade = shade_of(y, step)
                same_z, next_z = jnp.where(left, shade, 0.0), jnp.where(left, LOW, shade)
            if low:
                pieces.append(scores[start:middle])
            pieces.append(scores[middle:end] + same_z)
            pieces.append(scores[end : end + ROWS] + next_z)
        scores = jnp.concatenate(pieces, axis=0)
        if first:
            row_max = jnp.max(scores, axis=0, keepdims=True)
            weights = jnp.exp2((scores - row_max) * EXP2_SCALE)
            total = jnp.sum(weights, axis=0, keepdims=True)
            summed = jnp.dot(v_tile, weights.astype(BF16), preferred_element_type=F32)
        else:
            old = [
                jnp.concatenate([ref[z : z + 1, :] for z in (low, high)], axis=1)
                for ref in old_refs[:2]
            ] + [jnp.concatenate([old_refs[2][z] for z in (low, high)], axis=1)]
            row_max, total, summed = fold(old, scores, v_tile)
        for z, side in ((low, slice(0, ROWS)), (high, slice(ROWS, None))):
            if last:
                results[0][z] = (summed[:, side] * (1.0 / total[:, side])).astype(BF16)
            else:
                results[0][z : z + 1, :] = row_max[:, side]
                results[1][z : z + 1, :] = total[:, side]
                results[2][z] = summed[:, side]


def attend(y_index, own, steps, parts, state=(), last=False):
    rows = jax.ShapeDtypeStruct((ZS, ROWS), F32)
    kept = (rows, rows, jax.ShapeDtypeStruct((ZS, HD, ROWS), F32))
    share = len(steps)
    return pl.pallas_call(
        functools.partial(attend_kernel, steps, len(parts), not state, last),
        out_shape=jax.ShapeDtypeStruct((ZS, HD, ROWS), BF16) if last else kept,
        in_specs=[SMEM] + [VMEM] * (1 + len(parts) + len(state)),
        out_specs=VMEM if last else (VMEM,) * 3,
        scratch_shapes=[pltpu.VMEM((HD, 2 * ROWS), BF16)],
        compiler_params=params(),
        name="attend_far" if last else "attend_near",
        cost_estimate=pl.CostEstimate(
            flops=350_000_000 * share, bytes_accessed=1_500_000, transcendentals=650_000 * share
        ),
    )(y_index, own, *parts, *state)


def cross_kernel(ids0_ref, ids1_ref, place_ref, q0_ref, q1_ref, db_ref, out0_ref, out1_ref, *refs):
    top, total, summed, blocks, queries, arrived, ready = refs
    here = place_ref[0]
    fetches = [
        pltpu.make_async_copy(q_ref, queries.at[slot], arrived.at[slot])
        for slot, q_ref in enumerate((q0_ref, q1_ref))
    ]
    for fetch in fetches:
        fetch.start()

    def named(ids_ref, index):
        which, span, n = (index + 2) // 4, lax.rem(index // 2 + 1, 2), lax.rem(index, 2)
        return ids_ref[which, span, n, 0], ids_ref[which, span, n, 1]

    def fetch_block(block, place):
        return pltpu.make_async_copy(db_ref.at[:, block], blocks.at[place], ready.at[place])

    for slot, ids_ref in enumerate((ids0_ref, ids1_ref)):

        def request(index, carry, slot=slot, ids_ref=ids_ref):
            shard, block = named(ids_ref, index)

            @pl.when(shard == here)
            def _():
                fetch_block(block, 6 * slot + index).start()

            return carry

        lax.fori_loop(0, 6, request, 0)
    for fetch in fetches:
        fetch.wait()
    row = lax.broadcasted_iota(jnp.int32, (1, ROWS), 1)
    group_of = (row + 1) // 64
    for slot, ids_ref, out_ref in ((0, ids0_ref, out0_ref), (1, ids1_ref, out1_ref)):
        top[...] = jnp.full(top.shape, LOW, F32)
        total[...] = jnp.zeros(total.shape, F32)
        summed[...] = jnp.zeros(summed.shape, F32)

        def neighbour(index, carry, ids_ref=ids_ref, slot=slot):
            shard, block = named(ids_ref, index)
            place = 6 * slot + index

            @pl.when(shard == here)
            def _():
                fetch_block(block, place).wait()
                inside = group_of == index // 2
                cols = [slice(h * HD, (h + 1) * HD) for h in range(HEADS)]
                scores = [
                    lax.dot_general(
                        blocks[place, 0, :, c],
                        queries[slot, :, c],
                        (((1,), (1,)), ((), ())),
                        preferred_element_type=F32,
                    )
                    for c in cols
                ]
                old_max = top[...]
                new_max = jnp.concatenate(
                    [jnp.max(block_scores, axis=0, keepdims=True) for block_scores in scores], axis=0
                )
                new_max = jnp.where(inside, jnp.maximum(old_max, new_max), old_max)
                fade = jnp.exp2((old_max - new_max) * EXP2_SCALE)
                weights = [
                    jnp.where(
                        inside, jnp.exp2((scores[h] - new_max[h : h + 1]) * EXP2_SCALE), 0.0
                    )
                    for h in range(HEADS)
                ]
                sums = [jnp.sum(w, axis=0, keepdims=True) for w in weights]
                products = [
                    lax.dot_general(
                        blocks[place, 1, :, cols[h]],
                        weights[h].astype(BF16),
                        (((0,), (0,)), ((), ())),
                        preferred_element_type=F32,
                    )
                    for h in range(HEADS)
                ]
                top[...] = new_max
                total[...] = total[...] * fade + jnp.concatenate(sums, axis=0)
                for h in range(HEADS):
                    summed[h] = summed[h] * fade[h : h + 1] + products[h]

            return carry

        lax.fori_loop(0, 6, neighbour, 0)
        sums = total[...]
        some = sums > 0.0
        safe = jnp.where(some, sums, 1.0)
        inverse = 1.0 / safe
        for h in range(HEADS):
            out_ref[h * HD : (h + 1) * HD, :] = (summed[h] * inverse[h : h + 1, :]).astype(BF16)
        level = jnp.where(some, top[...] * EXP2_SCALE + jnp.log2(safe), LOW)
        store_level(out_ref, level)


def cross_attend(place, ids, queries, database):
    shape = jax.ShapeDtypeStruct((HEADS * HD + STAT, ROWS), BF16)
    return pl.pallas_call(
        cross_kernel,
        out_shape=(shape,) * 2,
        in_specs=[SMEM] * 3 + [pl.BlockSpec(memory_space=pl.ANY)] * 3,
        out_specs=(VMEM,) * 2,
        scratch_shapes=[
            pltpu.VMEM((HEADS, ROWS), F32),
            pltpu.VMEM((HEADS, ROWS), F32),
            pltpu.VMEM((HEADS, HD, ROWS), F32),
            pltpu.VMEM((12, 2, RETR, HEADS * HD), BF16),
            pltpu.VMEM((2, ROWS, HEADS * HD), BF16),
            pltpu.SemaphoreType.DMA((2,)),
            pltpu.SemaphoreType.DMA((12,)),
        ],
        compiler_params=params(56 * 1024 * 1024),
        name="cross_attend",
        cost_estimate=pl.CostEstimate(
            flops=2_000_000_000, bytes_accessed=5_000_000, transcendentals=1_000_000
        ),
    )(*ids, place, *queries, database)


def level_of(part_ref):
    stats = part_ref[HEADS * HD :, :].astype(F32)
    return stats[0:8] + stats[8:16] + stats[16:24]


def store_level(out_ref, level):
    high = level.astype(BF16).astype(F32)
    middle = (level - high).astype(BF16).astype(F32)
    low = level - high - middle
    stats = jnp.concatenate([high, middle, low, jnp.zeros_like(low)], axis=0)
    out_ref[HEADS * HD :, :] = stats.astype(BF16)


def merge_kernel(first_ref, second_ref, out_ref):
    levels = [level_of(first_ref), level_of(second_ref)]
    top = jnp.maximum(*levels)
    shares = [jnp.exp2(level - top) for level in levels]
    whole = shares[0] + shares[1]
    shares = [share / whole for share in shares]
    for h in range(HEADS):
        cols = slice(h * HD, (h + 1) * HD)
        first = first_ref[cols, :].astype(F32) * shares[0][h : h + 1, :]
        second = second_ref[cols, :].astype(F32) * shares[1][h : h + 1, :]
        out_ref[cols, :] = (first + second).astype(BF16)
    store_level(out_ref, top + jnp.log2(whole))


def merge(first, second):
    return pl.pallas_call(
        merge_kernel,
        out_shape=jax.ShapeDtypeStruct(first.shape, BF16),
        in_specs=[VMEM] * 2,
        out_specs=VMEM,
        compiler_params=params(),
        name="merge",
        cost_estimate=pl.CostEstimate(flops=0, bytes_accessed=800_000, transcendentals=4096),
    )(first, second)


COLS = 2048


def join_kernel(place_ref, self_ref, *refs):
    part_refs, att_ref = refs[0:3], refs[3]
    row = lax.broadcasted_iota(jnp.int32, (1, ROWS), 1)
    live = jnp.where((row >= 63) | (place_ref[0] > 0), 1.0, 0.0).astype(F32)
    levels = [level_of(part) for part in part_refs]
    top = functools.reduce(jnp.maximum, levels)
    shares = [jnp.exp2(level - top) for level in levels]
    whole = functools.reduce(jnp.add, shares)
    shares = [share / whole * live for share in shares]
    for h in range(HEADS):
        cols = slice(h * HD, (h + 1) * HD)
        joined = self_ref[h].astype(F32)
        for part, share in zip(part_refs, shares):
            joined = joined + part[cols, :].astype(F32) * share[h : h + 1, :]
        att_ref[:, cols] = jnp.transpose(joined).astype(BF16)


def join(place, self_parts, cross_parts):
    return pl.pallas_call(
        join_kernel,
        out_shape=jax.ShapeDtypeStruct((ROWS, HEADS * HD), BF16),
        in_specs=[SMEM] + [VMEM] * 4,
        out_specs=VMEM,
        compiler_params=params(),
        name="join",
        cost_estimate=pl.CostEstimate(flops=0, bytes_accessed=1_500_000, transcendentals=4096),
    )(place, self_parts, *cross_parts)


PIECES = 4


def add_kernel(kept0_ref, kept1_ref, received0_ref, received1_ref, out_ref, buffer, done):
    wide = COLS // PIECES
    copies = []
    for piece in range(PIECES):
        cols = slice(piece * wide, (piece + 1) * wide)
        kept_ref, received_ref = (
            (kept0_ref, received0_ref) if 2 * piece < PIECES else (kept1_ref, received1_ref)
        )
        inner = slice(cols.start % (COLS // 2), cols.start % (COLS // 2) + wide)
        kept, received = kept_ref[:, inner].astype(F32), received_ref[:, inner].astype(F32)
        buffer[:, cols] = (kept + received).astype(BF16)
        copies.append(
            pltpu.make_async_copy(buffer.at[:, cols], out_ref.at[:, cols], done.at[piece])
        )
        copies[-1].start()
    for copy in copies:
        copy.wait()


def add(kept, received):
    return pl.pallas_call(
        add_kernel,
        out_shape=jax.ShapeDtypeStruct((ROWS, COLS), BF16),
        in_specs=[VMEM] * 4,
        out_specs=pl.BlockSpec(memory_space=pl.ANY),
        scratch_shapes=[pltpu.VMEM((ROWS, COLS), BF16), pltpu.SemaphoreType.DMA((PIECES,))],
        compiler_params=params(),
        name="add",
        cost_estimate=pl.CostEstimate(flops=0, bytes_accessed=1_500_000, transcendentals=0),
    )(*kept, *received)


def ring(axis, step):
    count = lax.axis_size(axis)
    return [(i, (i + step) % count) for i in range(count)]


def per_device(queries, keys, values, cross_queries, neighbour_ids, database, out_weight):
    dp = ("xl", "core")
    seq = ("z", "y")
    seq_index = lax.axis_index(seq).astype(jnp.int32).reshape(1)
    y_index = lax.axis_index("y").astype(jnp.int32).reshape(1)
    place_dp = lax.axis_index(dp).astype(jnp.int32).reshape(1)
    across, beside = ring("xl", 1), ring("core", 1)
    up, down = ring("y", 1), ring("y", -1)

    earlier_ids = lax.ppermute(neighbour_ids, seq, [(i, i + 1) for i in range(ZS * YS - 1)])
    own = split_heads(queries[0], keys[0], values[0])
    own, earlier_ids = lax.optimization_barrier((own, earlier_ids))
    own = lax.all_to_all(own, "z", 0, 0, tiled=True)

    mine = cross_queries[0]
    ids = jnp.concatenate([earlier_ids, neighbour_ids], axis=0)
    from_across = lax.ppermute(mine, "xl", across)
    from_beside = lax.ppermute(mine, "core", beside)
    ids_across = lax.ppermute(ids, "xl", across)
    ids_beside = lax.ppermute(ids, "core", beside)
    own_part, beside_part = cross_attend(
        place_dp, (ids, ids_beside), (mine, from_beside), database[0]
    )
    from_across, ids_across, _ = lax.optimization_barrier((from_across, ids_across, own_part))
    from_diagonal = lax.ppermute(from_across, "core", beside)
    ids_diagonal = lax.ppermute(ids_across, "core", beside)
    across_part, diagonal_part = cross_attend(
        place_dp, (ids_across, ids_diagonal), (from_across, from_diagonal), database[0]
    )
    beside_part = lax.ppermute(beside_part, "core", beside)
    diagonal_part = lax.ppermute(diagonal_part, "core", beside)
    own, _, _ = lax.optimization_barrier((own, across_part, beside_part))

    half = ZS // 2
    kv_low, kv_high = own[:half, :2], own[half:, :2]
    below_low = lax.ppermute(kv_low, "y", up)
    above_high = lax.ppermute(kv_high, "y", down)
    below_high = lax.ppermute(kv_high, "y", up)
    above_low = lax.ppermute(kv_low, "y", down)
    across_part = merge(across_part, diagonal_part)
    below_low, above_high, own, across_part = lax.optimization_barrier(
        (below_low, above_high, own, across_part)
    )

    far_low = lax.ppermute(below_low, "y", up)
    far_high = lax.ppermute(above_high, "y", down)
    across_part = lax.ppermute(across_part, "xl", across)
    state = attend(y_index, own, (0,), (own,))
    near = (below_low, below_high, above_low, above_high)
    state = attend(y_index, own, (YS - 1, 1), near, state)
    far_low, far_high, state, across_part = lax.optimization_barrier(
        (far_low, far_high, state, across_part)
    )

    self_t = attend(y_index, own, (2,), (far_low, far_high), state, last=True)
    self_t = lax.all_to_all(self_t, "z", 0, 0, tiled=True)

    attended = join(seq_index, self_t, (own_part, beside_part, across_part))
    xh = lax.axis_index("xh")

    def projected(half):
        columns = lax.dynamic_slice_in_dim(out_weight, half * (COLS // 2), COLS // 2, axis=1)
        return jnp.dot(attended, columns, preferred_element_type=F32).astype(BF16)

    received = [
        lax.ppermute(projected(2 * (1 - xh) + piece), "xh", ring("xh", 1)) for piece in range(2)
    ]
    return add([projected(2 * xh + piece) for piece in range(2)], received)[None]


def solution(mesh):
    split = Mesh(mesh.devices.reshape(2, 2, ZS, YS, 2), ("xl", "core", "z", "y", "xh"))
    dp, seq = ("xl", "core"), ("z", "y")
    placed = (
        P(dp, seq, "xh"),
        P(dp, seq, "xh"),
        P(dp, seq, "xh"),
        P(dp, seq, "xh"),
        P(dp, seq, None, None),
        P(dp, None, None, None, "xh"),
        P("xh", None),
    )
    return jax.shard_map(
        per_device, mesh=split, in_specs=placed, out_specs=P(dp, seq, "xh"), check_vma=False
    )
```

```python
import functools
import math

import jax
import jax.numpy as jnp
from jax import lax
from jax.experimental import pallas as pl
from jax.experimental.pallas import tpu as pltpu
from jax.sharding import Mesh, PartitionSpec as P

HD = 128
ROWS = 128
HEADS = 8
ZS, YS = 8, 4
RETR = 128
STAT = 32
LOW = -1e30
EXP2_SCALE = math.log2(math.e) / math.sqrt(HD)
VMEM_LIMIT = 24 * 1024 * 1024

VMEM = pl.BlockSpec(memory_space=pltpu.VMEM)
SMEM = pl.BlockSpec(memory_space=pltpu.SMEM)
F32 = jnp.float32
BF16 = jnp.bfloat16


def params(limit=VMEM_LIMIT):
    return pltpu.CompilerParams(vmem_limit_bytes=limit)


def flipped(block):
    return jnp.transpose(block.astype(F32)).astype(BF16)


def split_kernel(q_ref, k_ref, v_ref, out_ref):
    for h in range(HEADS):
        cols = pl.ds(h * HD, HD)
        out_ref[h, 0] = k_ref[:, cols]
        out_ref[h, 1] = flipped(v_ref[:, cols])
        out_ref[h, 2] = flipped(q_ref[:, cols])


def split_heads(queries, keys, values):
    return pl.pallas_call(
        split_kernel,
        out_shape=jax.ShapeDtypeStruct((HEADS, 3, ROWS, HD), BF16),
        in_specs=[VMEM] * 3,
        out_specs=VMEM,
        compiler_params=params(56 * 1024 * 1024),
        name="split_heads",
        cost_estimate=pl.CostEstimate(flops=0, bytes_accessed=1536 * 1024, transcendentals=0),
    )(queries, keys, values)


def shade_of(y, step):
    return jnp.where(lax.rem(y + step, YS) < y, 0.0, LOW).astype(F32)


def fold(state, scores, v_tile):
    row_max, total, summed = state
    new_max = jnp.maximum(row_max, jnp.max(scores, axis=0, keepdims=True))
    weights = jnp.exp2((scores - new_max) * EXP2_SCALE)
    fade = jnp.exp2((row_max - new_max) * EXP2_SCALE)
    total = total * fade + jnp.sum(weights, axis=0, keepdims=True)
    summed = summed * fade + jnp.dot(v_tile, weights.astype(BF16), preferred_element_type=F32)
    return new_max, total, summed


def attend_kernel(steps, count, first, last, y_ref, own_ref, *refs):
    part_refs, refs = refs[:count], refs[count:]
    if not first:
        old_refs, refs = refs[:3], refs[3:]
    wide, results = refs[-1], refs[:-1]
    y = y_ref[0]
    left = lax.broadcasted_iota(jnp.int32, (1, 2 * ROWS), 1) < ROWS
    key_pos = lax.broadcasted_iota(jnp.int32, (ROWS, 2 * ROWS), 0)
    query_pos = lax.broadcasted_iota(jnp.int32, (ROWS, 2 * ROWS), 1)
    halves = count // len(steps)

    def block(part, z, kind):
        depth = ZS // halves
        return part_refs[part * halves + z // depth][z % depth, kind]

    for pair in range(ZS // 2):
        low, high = 2 * pair, 2 * pair + 1
        wide[:, 0:ROWS] = own_ref[low, 2]
        wide[:, ROWS:] = own_ref[high, 2]
        places = [(part, z) for part in range(len(steps)) for z in range(high + 1)]
        k_tile = jnp.concatenate([block(part, z, 0) for part, z in places], axis=0)
        v_tile = jnp.concatenate([block(part, z, 1) for part, z in places], axis=1)
        scores = jnp.dot(k_tile, wide[...], preferred_element_type=F32)
        pieces = []
        for part, step in enumerate(steps):
            start = part * (high + 1) * ROWS
            middle, end = start + low * ROWS, start + high * ROWS
            if step == 0:
                same_z = jnp.where(left & (key_pos > query_pos), LOW, 0.0)
                next_z = jnp.where(left | (key_pos > query_pos - ROWS), LOW, 0.0)
            else:
                shade = shade_of(y, step)
                same_z, next_z = jnp.where(left, shade, 0.0), jnp.where(left, LOW, shade)
            if low:
                pieces.append(scores[start:middle])
            pieces.append(scores[middle:end] + same_z)
            pieces.append(scores[end : end + ROWS] + next_z)
        scores = jnp.concatenate(pieces, axis=0)
        if first:
            row_max = jnp.max(scores, axis=0, keepdims=True)
            weights = jnp.exp2((scores - row_max) * EXP2_SCALE)
            total = jnp.sum(weights, axis=0, keepdims=True)
            summed = jnp.dot(v_tile, weights.astype(BF16), preferred_element_type=F32)
        else:
            old = [
                jnp.concatenate([ref[z : z + 1, :] for z in (low, high)], axis=1)
                for ref in old_refs[:2]
            ] + [jnp.concatenate([old_refs[2][z] for z in (low, high)], axis=1)]
            row_max, total, summed = fold(old, scores, v_tile)
        for z, side in ((low, slice(0, ROWS)), (high, slice(ROWS, None))):
            if last:
                results[0][z] = (summed[:, side] * (1.0 / total[:, side])).astype(BF16)
            else:
                results[0][z : z + 1, :] = row_max[:, side]
                results[1][z : z + 1, :] = total[:, side]
                results[2][z] = summed[:, side]


def attend(y_index, own, steps, parts, state=(), last=False):
    rows = jax.ShapeDtypeStruct((ZS, ROWS), F32)
    kept = (rows, rows, jax.ShapeDtypeStruct((ZS, HD, ROWS), F32))
    share = len(steps)
    return pl.pallas_call(
        functools.partial(attend_kernel, steps, len(parts), not state, last),
        out_shape=jax.ShapeDtypeStruct((ZS, HD, ROWS), BF16) if last else kept,
        in_specs=[SMEM] + [VMEM] * (1 + len(parts) + len(state)),
        out_specs=VMEM if last else (VMEM,) * 3,
        scratch_shapes=[pltpu.VMEM((HD, 2 * ROWS), BF16)],
        compiler_params=params(),
        name="attend_far" if last else "attend_near",
        cost_estimate=pl.CostEstimate(
            flops=350_000_000 * share, bytes_accessed=1_500_000, transcendentals=650_000 * share
        ),
    )(y_index, own, *parts, *state)


def cross_kernel(ids0_ref, ids1_ref, place_ref, q0_ref, q1_ref, db_ref, out0_ref, out1_ref, *refs):
    top, total, summed, blocks, ready = refs
    here = place_ref[0]

    def named(ids_ref, index):
        which, span, n = (index + 2) // 4, lax.rem(index // 2 + 1, 2), lax.rem(index, 2)
        return ids_ref[which, span, n, 0], ids_ref[which, span, n, 1]

    def fetch_block(block, place):
        return pltpu.make_async_copy(db_ref.at[:, block], blocks.at[place], ready.at[place])

    for slot, ids_ref in enumerate((ids0_ref, ids1_ref)):

        def request(index, carry, slot=slot, ids_ref=ids_ref):
            shard, block = named(ids_ref, index)

            @pl.when(shard == here)
            def _():
                fetch_block(block, 6 * slot + index).start()

            return carry

        lax.fori_loop(0, 6, request, 0)
    row = lax.broadcasted_iota(jnp.int32, (1, ROWS), 1)
    group_of = (row + 1) // 64
    for slot, ids_ref, q_ref, out_ref in (
        (0, ids0_ref, q0_ref, out0_ref),
        (1, ids1_ref, q1_ref, out1_ref),
    ):
        top[...] = jnp.full(top.shape, LOW, F32)
        total[...] = jnp.zeros(total.shape, F32)
        summed[...] = jnp.zeros(summed.shape, F32)

        def neighbour(index, carry, slot=slot, ids_ref=ids_ref, q_ref=q_ref):
            shard, block = named(ids_ref, index)
            place = 6 * slot + index

            @pl.when(shard == here)
            def _():
                fetch_block(block, place).wait()
                inside = group_of == index // 2
                cols = [slice(h * HD, (h + 1) * HD) for h in range(HEADS)]
                scores = [
                    lax.dot_general(
                        blocks[place, 0, :, c],
                        q_ref[:, c],
                        (((1,), (1,)), ((), ())),
                        preferred_element_type=F32,
                    )
                    for c in cols
                ]
                old_max = top[...]
                new_max = jnp.concatenate(
                    [jnp.max(block_scores, axis=0, keepdims=True) for block_scores in scores], axis=0
                )
                new_max = jnp.where(inside, jnp.maximum(old_max, new_max), old_max)
                fade = jnp.exp2((old_max - new_max) * EXP2_SCALE)
                weights = [
                    jnp.where(
                        inside, jnp.exp2((scores[h] - new_max[h : h + 1]) * EXP2_SCALE), 0.0
                    )
                    for h in range(HEADS)
                ]
                sums = [jnp.sum(w, axis=0, keepdims=True) for w in weights]
                products = [
                    lax.dot_general(
                        blocks[place, 1, :, cols[h]],
                        weights[h].astype(BF16),
                        (((0,), (0,)), ((), ())),
                        preferred_element_type=F32,
                    )
                    for h in range(HEADS)
                ]
                top[...] = new_max
                total[...] = total[...] * fade + jnp.concatenate(sums, axis=0)
                for h in range(HEADS):
                    summed[h] = summed[h] * fade[h : h + 1] + products[h]

            return carry

        lax.fori_loop(0, 6, neighbour, 0)
        sums = total[...]
        some = sums > 0.0
        safe = jnp.where(some, sums, 1.0)
        inverse = 1.0 / safe
        for h in range(HEADS):
            out_ref[h * HD : (h + 1) * HD, :] = (summed[h] * inverse[h : h + 1, :]).astype(BF16)
        level = jnp.where(some, top[...] * EXP2_SCALE + jnp.log2(safe), LOW)
        store_level(out_ref, level)


def cross_attend(place, ids, queries, database):
    shape = jax.ShapeDtypeStruct((HEADS * HD + STAT, ROWS), BF16)
    return pl.pallas_call(
        cross_kernel,
        out_shape=(shape,) * 2,
        in_specs=[SMEM] * 3 + [VMEM] * 2 + [pl.BlockSpec(memory_space=pl.ANY)],
        out_specs=(VMEM,) * 2,
        scratch_shapes=[
            pltpu.VMEM((HEADS, ROWS), F32),
            pltpu.VMEM((HEADS, ROWS), F32),
            pltpu.VMEM((HEADS, HD, ROWS), F32),
            pltpu.VMEM((12, 2, RETR, HEADS * HD), BF16),
            pltpu.SemaphoreType.DMA((12,)),
        ],
        compiler_params=params(52 * 1024 * 1024),
        name="cross_attend",
        cost_estimate=pl.CostEstimate(
            flops=2_000_000_000, bytes_accessed=5_000_000, transcendentals=1_000_000
        ),
    )(*ids, place, *queries, database)


def level_of(part_ref):
    stats = part_ref[HEADS * HD :, :].astype(F32)
    return stats[0:8] + stats[8:16] + stats[16:24]


def store_level(out_ref, level):
    high = level.astype(BF16).astype(F32)
    middle = (level - high).astype(BF16).astype(F32)
    low = level - high - middle
    stats = jnp.concatenate([high, middle, low, jnp.zeros_like(low)], axis=0)
    out_ref[HEADS * HD :, :] = stats.astype(BF16)


def merge_kernel(first_ref, second_ref, out_ref):
    levels = [level_of(first_ref), level_of(second_ref)]
    top = jnp.maximum(*levels)
    shares = [jnp.exp2(level - top) for level in levels]
    whole = shares[0] + shares[1]
    shares = [share / whole for share in shares]
    for h in range(HEADS):
        cols = slice(h * HD, (h + 1) * HD)
        first = first_ref[cols, :].astype(F32) * shares[0][h : h + 1, :]
        second = second_ref[cols, :].astype(F32) * shares[1][h : h + 1, :]
        out_ref[cols, :] = (first + second).astype(BF16)
    store_level(out_ref, top + jnp.log2(whole))


def merge(first, second):
    return pl.pallas_call(
        merge_kernel,
        out_shape=jax.ShapeDtypeStruct(first.shape, BF16),
        in_specs=[VMEM] * 2,
        out_specs=VMEM,
        compiler_params=params(),
        name="merge",
        cost_estimate=pl.CostEstimate(flops=0, bytes_accessed=800_000, transcendentals=4096),
    )(first, second)


COLS = 2048


def join_kernel(place_ref, self_ref, *refs):
    part_refs, att_ref = refs[0:3], refs[3]
    row = lax.broadcasted_iota(jnp.int32, (1, ROWS), 1)
    live = jnp.where((row >= 63) | (place_ref[0] > 0), 1.0, 0.0).astype(F32)
    levels = [level_of(part) for part in part_refs]
    top = functools.reduce(jnp.maximum, levels)
    shares = [jnp.exp2(level - top) for level in levels]
    whole = functools.reduce(jnp.add, shares)
    shares = [share / whole * live for share in shares]
    for h in range(HEADS):
        cols = slice(h * HD, (h + 1) * HD)
        joined = self_ref[h].astype(F32)
        for part, share in zip(part_refs, shares):
            joined = joined + part[cols, :].astype(F32) * share[h : h + 1, :]
        att_ref[:, cols] = jnp.transpose(joined).astype(BF16)


def join(place, self_parts, cross_parts):
    return pl.pallas_call(
        join_kernel,
        out_shape=jax.ShapeDtypeStruct((ROWS, HEADS * HD), BF16),
        in_specs=[SMEM] + [VMEM] * 4,
        out_specs=VMEM,
        compiler_params=params(),
        name="join",
        cost_estimate=pl.CostEstimate(flops=0, bytes_accessed=1_500_000, transcendentals=4096),
    )(place, self_parts, *cross_parts)


PIECES = 4


def add_kernel(kept0_ref, kept1_ref, received0_ref, received1_ref, out_ref, buffer, done):
    wide = COLS // PIECES
    copies = []
    for piece in range(PIECES):
        cols = slice(piece * wide, (piece + 1) * wide)
        kept_ref, received_ref = (
            (kept0_ref, received0_ref) if 2 * piece < PIECES else (kept1_ref, received1_ref)
        )
        inner = slice(cols.start % (COLS // 2), cols.start % (COLS // 2) + wide)
        kept, received = kept_ref[:, inner].astype(F32), received_ref[:, inner].astype(F32)
        buffer[:, cols] = (kept + received).astype(BF16)
        copies.append(
            pltpu.make_async_copy(buffer.at[:, cols], out_ref.at[:, cols], done.at[piece])
        )
        copies[-1].start()
    for copy in copies:
        copy.wait()


def add(kept, received):
    return pl.pallas_call(
        add_kernel,
        out_shape=jax.ShapeDtypeStruct((ROWS, COLS), BF16),
        in_specs=[VMEM] * 4,
        out_specs=pl.BlockSpec(memory_space=pl.ANY),
        scratch_shapes=[pltpu.VMEM((ROWS, COLS), BF16), pltpu.SemaphoreType.DMA((PIECES,))],
        compiler_params=params(),
        name="add",
        cost_estimate=pl.CostEstimate(flops=0, bytes_accessed=1_500_000, transcendentals=0),
    )(*kept, *received)


def ring(axis, step):
    count = lax.axis_size(axis)
    return [(i, (i + step) % count) for i in range(count)]


def per_device(queries, keys, values, cross_queries, neighbour_ids, database, out_weight):
    dp = ("xl", "core")
    seq = ("z", "y")
    seq_index = lax.axis_index(seq).astype(jnp.int32).reshape(1)
    y_index = lax.axis_index("y").astype(jnp.int32).reshape(1)
    place_dp = lax.axis_index(dp).astype(jnp.int32).reshape(1)
    across, beside = ring("xl", 1), ring("core", 1)
    up, down = ring("y", 1), ring("y", -1)

    earlier_ids = lax.ppermute(neighbour_ids, seq, [(i, i + 1) for i in range(ZS * YS - 1)])
    own = split_heads(queries[0], keys[0], values[0])
    own, earlier_ids = lax.optimization_barrier((own, earlier_ids))
    own = lax.all_to_all(own, "z", 0, 0, tiled=True)

    mine = cross_queries[0]
    ids = jnp.concatenate([earlier_ids, neighbour_ids], axis=0)
    from_across = lax.ppermute(mine, "xl", across)
    from_beside = lax.ppermute(mine, "core", beside)
    ids_across = lax.ppermute(ids, "xl", across)
    ids_beside = lax.ppermute(ids, "core", beside)
    own_part, beside_part = cross_attend(
        place_dp, (ids, ids_beside), (mine, from_beside), database[0]
    )
    from_across, ids_across, _ = lax.optimization_barrier((from_across, ids_across, own_part))
    from_diagonal = lax.ppermute(from_across, "core", beside)
    ids_diagonal = lax.ppermute(ids_across, "core", beside)
    across_part, diagonal_part = cross_attend(
        place_dp, (ids_across, ids_diagonal), (from_across, from_diagonal), database[0]
    )
    beside_part = lax.ppermute(beside_part, "core", beside)
    diagonal_part = lax.ppermute(diagonal_part, "core", beside)
    own, _, _ = lax.optimization_barrier((own, across_part, beside_part))

    half = ZS // 2
    kv_low, kv_high = own[:half, :2], own[half:, :2]
    below_low = lax.ppermute(kv_low, "y", up)
    above_high = lax.ppermute(kv_high, "y", down)
    below_high = lax.ppermute(kv_high, "y", up)
    above_low = lax.ppermute(kv_low, "y", down)
    across_part = merge(across_part, diagonal_part)
    below_low, above_high, own, _ = lax.optimization_barrier(
        (below_low, above_high, own, across_part)
    )

    far_low = lax.ppermute(below_low, "y", up)
    far_high = lax.ppermute(above_high, "y", down)
    across_part = lax.ppermute(across_part, "xl", across)
    state = attend(y_index, own, (0,), (own,))
    near = (below_low, below_high, above_low, above_high)
    state = attend(y_index, own, (YS - 1, 1), near, state)
    far_low, far_high, state, across_part = lax.optimization_barrier(
        (far_low, far_high, state, across_part)
    )

    self_t = attend(y_index, own, (2,), (far_low, far_high), state, last=True)
    self_t = lax.all_to_all(self_t, "z", 0, 0, tiled=True)

    attended = join(seq_index, self_t, (own_part, beside_part, across_part))
    xh = lax.axis_index("xh")

    def projected(half):
        columns = lax.dynamic_slice_in_dim(out_weight, half * (COLS // 2), COLS // 2, axis=1)
        return jnp.dot(attended, columns, preferred_element_type=F32).astype(BF16)

    received = [
        lax.ppermute(projected(2 * (1 - xh) + piece), "xh", ring("xh", 1)) for piece in range(2)
    ]
    return add([projected(2 * xh + piece) for piece in range(2)], received)[None]


def solution(mesh):
    split = Mesh(mesh.devices.reshape(2, 2, ZS, YS, 2), ("xl", "core", "z", "y", "xh"))
    dp, seq = ("xl", "core"), ("z", "y")
    placed = (
        P(dp, seq, "xh"),
        P(dp, seq, "xh"),
        P(dp, seq, "xh"),
        P(dp, seq, "xh"),
        P(dp, seq, None, None),
        P(dp, None, None, None, "xh"),
        P("xh", None),
    )
    return jax.shard_map(
        per_device, mesh=split, in_specs=placed, out_specs=P(dp, seq, "xh"), check_vma=False
    )
```

```python
import functools
import math

import jax
import jax.numpy as jnp
from jax import lax
from jax.experimental import pallas as pl
from jax.experimental.pallas import tpu as pltpu
from jax.sharding import Mesh, PartitionSpec as P

HD = 128
ROWS = 128
HEADS = 8
ZS, YS = 8, 4
RETR = 128
STAT = 32
LOW = -1e30
EXP2_SCALE = math.log2(math.e) / math.sqrt(HD)
VMEM_LIMIT = 24 * 1024 * 1024

VMEM = pl.BlockSpec(memory_space=pltpu.VMEM)
SMEM = pl.BlockSpec(memory_space=pltpu.SMEM)
F32 = jnp.float32
BF16 = jnp.bfloat16


def params(limit=VMEM_LIMIT):
    return pltpu.CompilerParams(vmem_limit_bytes=limit)


def flipped(block):
    return jnp.transpose(block.astype(F32)).astype(BF16)


def split_kernel(q_ref, k_ref, v_ref, out_ref):
    for h in range(HEADS):
        cols = pl.ds(h * HD, HD)
        out_ref[h, 0] = k_ref[:, cols]
        out_ref[h, 1] = flipped(v_ref[:, cols])
        out_ref[h, 2] = flipped(q_ref[:, cols])


def split_heads(queries, keys, values):
    return pl.pallas_call(
        split_kernel,
        out_shape=jax.ShapeDtypeStruct((HEADS, 3, ROWS, HD), BF16),
        in_specs=[VMEM] * 3,
        out_specs=VMEM,
        compiler_params=params(56 * 1024 * 1024),
        name="split_heads",
        cost_estimate=pl.CostEstimate(flops=0, bytes_accessed=1536 * 1024, transcendentals=0),
    )(queries, keys, values)


def shade_of(y, step):
    return jnp.where(lax.rem(y + step, YS) < y, 0.0, LOW).astype(F32)


def fold(state, scores, v_tile):
    row_max, total, summed = state
    new_max = jnp.maximum(row_max, jnp.max(scores, axis=0, keepdims=True))
    weights = jnp.exp2((scores - new_max) * EXP2_SCALE)
    fade = jnp.exp2((row_max - new_max) * EXP2_SCALE)
    total = total * fade + jnp.sum(weights, axis=0, keepdims=True)
    summed = summed * fade + jnp.dot(v_tile, weights.astype(BF16), preferred_element_type=F32)
    return new_max, total, summed


def attend_kernel(steps, count, first, last, y_ref, own_ref, *refs):
    part_refs, refs = refs[:count], refs[count:]
    if not first:
        old_refs, refs = refs[:3], refs[3:]
    wide, results = refs[-1], refs[:-1]
    y = y_ref[0]
    left = lax.broadcasted_iota(jnp.int32, (1, 2 * ROWS), 1) < ROWS
    key_pos = lax.broadcasted_iota(jnp.int32, (ROWS, 2 * ROWS), 0)
    query_pos = lax.broadcasted_iota(jnp.int32, (ROWS, 2 * ROWS), 1)
    halves = count // len(steps)

    def block(part, z, kind):
        depth = ZS // halves
        return part_refs[part * halves + z // depth][z % depth, kind]

    for pair in range(ZS // 2):
        low, high = 2 * pair, 2 * pair + 1
        wide[:, 0:ROWS] = own_ref[low, 2]
        wide[:, ROWS:] = own_ref[high, 2]
        places = [(part, z) for part in range(len(steps)) for z in range(high + 1)]
        k_tile = jnp.concatenate([block(part, z, 0) for part, z in places], axis=0)
        v_tile = jnp.concatenate([block(part, z, 1) for part, z in places], axis=1)
        scores = jnp.dot(k_tile, wide[...], preferred_element_type=F32)
        pieces = []
        for part, step in enumerate(steps):
            start = part * (high + 1) * ROWS
            middle, end = start + low * ROWS, start + high * ROWS
            if step == 0:
                same_z = jnp.where(left & (key_pos > query_pos), LOW, 0.0)
                next_z = jnp.where(left | (key_pos > query_pos - ROWS), LOW, 0.0)
            else:
                shade = shade_of(y, step)
                same_z, next_z = jnp.where(left, shade, 0.0), jnp.where(left, LOW, shade)
            if low:
                pieces.append(scores[start:middle])
            pieces.append(scores[middle:end] + same_z)
            pieces.append(scores[end : end + ROWS] + next_z)
        scores = jnp.concatenate(pieces, axis=0)
        if first:
            row_max = jnp.max(scores, axis=0, keepdims=True)
            weights = jnp.exp2((scores - row_max) * EXP2_SCALE)
            total = jnp.sum(weights, axis=0, keepdims=True)
            summed = jnp.dot(v_tile, weights.astype(BF16), preferred_element_type=F32)
        else:
            old = [
                jnp.concatenate([ref[z : z + 1, :] for z in (low, high)], axis=1)
                for ref in old_refs[:2]
            ] + [jnp.concatenate([old_refs[2][z] for z in (low, high)], axis=1)]
            row_max, total, summed = fold(old, scores, v_tile)
        for z, side in ((low, slice(0, ROWS)), (high, slice(ROWS, None))):
            if last:
                results[0][z] = (summed[:, side] * (1.0 / total[:, side])).astype(BF16)
            else:
                results[0][z : z + 1, :] = row_max[:, side]
                results[1][z : z + 1, :] = total[:, side]
                results[2][z] = summed[:, side]


def attend(y_index, own, steps, parts, state=(), last=False):
    rows = jax.ShapeDtypeStruct((ZS, ROWS), F32)
    kept = (rows, rows, jax.ShapeDtypeStruct((ZS, HD, ROWS), F32))
    share = len(steps)
    return pl.pallas_call(
        functools.partial(attend_kernel, steps, len(parts), not state, last),
        out_shape=jax.ShapeDtypeStruct((ZS, HD, ROWS), BF16) if last else kept,
        in_specs=[SMEM] + [VMEM] * (1 + len(parts) + len(state)),
        out_specs=VMEM if last else (VMEM,) * 3,
        scratch_shapes=[pltpu.VMEM((HD, 2 * ROWS), BF16)],
        compiler_params=params(),
        name="attend_far" if last else "attend_near",
        cost_estimate=pl.CostEstimate(
            flops=350_000_000 * share, bytes_accessed=1_500_000, transcendentals=650_000 * share
        ),
    )(y_index, own, *parts, *state)


def cross_kernel(ids0_ref, ids1_ref, place_ref, q0_ref, q1_ref, db_ref, out0_ref, out1_ref, *refs):
    top, total, summed, blocks, ready = refs
    here = place_ref[0]

    def named(ids_ref, index):
        which, span, n = (index + 2) // 4, lax.rem(index // 2 + 1, 2), lax.rem(index, 2)
        return ids_ref[which, span, n, 0], ids_ref[which, span, n, 1]

    def fetch_block(block, place):
        return pltpu.make_async_copy(db_ref.at[:, block], blocks.at[place], ready.at[place])

    for slot, ids_ref in enumerate((ids0_ref, ids1_ref)):

        def request(index, carry, slot=slot, ids_ref=ids_ref):
            shard, block = named(ids_ref, index)

            @pl.when(shard == here)
            def _():
                fetch_block(block, 6 * slot + index).start()

            return carry

        lax.fori_loop(0, 6, request, 0)
    row = lax.broadcasted_iota(jnp.int32, (1, ROWS), 1)
    group_of = (row + 1) // 64
    for slot, ids_ref, q_ref, out_ref in (
        (0, ids0_ref, q0_ref, out0_ref),
        (1, ids1_ref, q1_ref, out1_ref),
    ):
        top[...] = jnp.full(top.shape, LOW, F32)
        total[...] = jnp.zeros(total.shape, F32)
        summed[...] = jnp.zeros(summed.shape, F32)

        def neighbour(index, carry, slot=slot, ids_ref=ids_ref, q_ref=q_ref):
            shard, block = named(ids_ref, index)
            place = 6 * slot + index

            @pl.when(shard == here)
            def _():
                fetch_block(block, place).wait()
                inside = group_of == index // 2
                cols = [slice(h * HD, (h + 1) * HD) for h in range(HEADS)]
                scores = [
                    lax.dot_general(
                        blocks[place, 0, :, c],
                        q_ref[:, c],
                        (((1,), (1,)), ((), ())),
                        preferred_element_type=F32,
                    )
                    for c in cols
                ]
                old_max = top[...]
                new_max = jnp.concatenate(
                    [jnp.max(block_scores, axis=0, keepdims=True) for block_scores in scores], axis=0
                )
                new_max = jnp.where(inside, jnp.maximum(old_max, new_max), old_max)
                fade = jnp.exp2((old_max - new_max) * EXP2_SCALE)
                weights = [
                    jnp.where(
                        inside, jnp.exp2((scores[h] - new_max[h : h + 1]) * EXP2_SCALE), 0.0
                    )
                    for h in range(HEADS)
                ]
                sums = [jnp.sum(w, axis=0, keepdims=True) for w in weights]
                products = [
                    lax.dot_general(
                        blocks[place, 1, :, cols[h]],
                        weights[h].astype(BF16),
                        (((0,), (0,)), ((), ())),
                        preferred_element_type=F32,
                    )
                    for h in range(HEADS)
                ]
                top[...] = new_max
                total[...] = total[...] * fade + jnp.concatenate(sums, axis=0)
                for h in range(HEADS):
                    summed[h] = summed[h] * fade[h : h + 1] + products[h]

            return carry

        lax.fori_loop(0, 6, neighbour, 0)
        sums = total[...]
        some = sums > 0.0
        safe = jnp.where(some, sums, 1.0)
        inverse = 1.0 / safe
        for h in range(HEADS):
            out_ref[h * HD : (h + 1) * HD, :] = (summed[h] * inverse[h : h + 1, :]).astype(BF16)
        level = jnp.where(some, top[...] * EXP2_SCALE + jnp.log2(safe), LOW)
        store_level(out_ref, level)


def cross_attend(place, ids, queries, database):
    shape = jax.ShapeDtypeStruct((HEADS * HD + STAT, ROWS), BF16)
    return pl.pallas_call(
        cross_kernel,
        out_shape=(shape,) * 2,
        in_specs=[SMEM] * 3 + [VMEM] * 2 + [pl.BlockSpec(memory_space=pl.ANY)],
        out_specs=(VMEM,) * 2,
        scratch_shapes=[
            pltpu.VMEM((HEADS, ROWS), F32),
            pltpu.VMEM((HEADS, ROWS), F32),
            pltpu.VMEM((HEADS, HD, ROWS), F32),
            pltpu.VMEM((12, 2, RETR, HEADS * HD), BF16),
            pltpu.SemaphoreType.DMA((12,)),
        ],
        compiler_params=params(52 * 1024 * 1024),
        name="cross_attend",
        cost_estimate=pl.CostEstimate(
            flops=2_000_000_000, bytes_accessed=5_000_000, transcendentals=1_000_000
        ),
    )(*ids, place, *queries, database)


def level_of(part_ref):
    stats = part_ref[HEADS * HD :, :].astype(F32)
    return stats[0:8] + stats[8:16] + stats[16:24]


def store_level(out_ref, level):
    high = level.astype(BF16).astype(F32)
    middle = (level - high).astype(BF16).astype(F32)
    low = level - high - middle
    stats = jnp.concatenate([high, middle, low, jnp.zeros_like(low)], axis=0)
    out_ref[HEADS * HD :, :] = stats.astype(BF16)


def merge_kernel(first_ref, second_ref, out_ref):
    levels = [level_of(first_ref), level_of(second_ref)]
    top = jnp.maximum(*levels)
    shares = [jnp.exp2(level - top) for level in levels]
    whole = shares[0] + shares[1]
    shares = [share / whole for share in shares]
    for h in range(HEADS):
        cols = slice(h * HD, (h + 1) * HD)
        first = first_ref[cols, :].astype(F32) * shares[0][h : h + 1, :]
        second = second_ref[cols, :].astype(F32) * shares[1][h : h + 1, :]
        out_ref[cols, :] = (first + second).astype(BF16)
    store_level(out_ref, top + jnp.log2(whole))


def merge(first, second):
    return pl.pallas_call(
        merge_kernel,
        out_shape=jax.ShapeDtypeStruct(first.shape, BF16),
        in_specs=[VMEM] * 2,
        out_specs=VMEM,
        compiler_params=params(),
        name="merge",
        cost_estimate=pl.CostEstimate(flops=0, bytes_accessed=800_000, transcendentals=4096),
    )(first, second)


COLS = 2048


def join_kernel(place_ref, self_ref, *refs):
    part_refs, att_ref = refs[0:3], refs[3]
    row = lax.broadcasted_iota(jnp.int32, (1, ROWS), 1)
    live = jnp.where((row >= 63) | (place_ref[0] > 0), 1.0, 0.0).astype(F32)
    levels = [level_of(part) for part in part_refs]
    top = functools.reduce(jnp.maximum, levels)
    shares = [jnp.exp2(level - top) for level in levels]
    whole = functools.reduce(jnp.add, shares)
    shares = [share / whole * live for share in shares]
    for h in range(HEADS):
        cols = slice(h * HD, (h + 1) * HD)
        joined = self_ref[h].astype(F32)
        for part, share in zip(part_refs, shares):
            joined = joined + part[cols, :].astype(F32) * share[h : h + 1, :]
        att_ref[:, cols] = jnp.transpose(joined).astype(BF16)


def join(place, self_parts, cross_parts):
    return pl.pallas_call(
        join_kernel,
        out_shape=jax.ShapeDtypeStruct((ROWS, HEADS * HD), BF16),
        in_specs=[SMEM] + [VMEM] * 4,
        out_specs=VMEM,
        compiler_params=params(),
        name="join",
        cost_estimate=pl.CostEstimate(flops=0, bytes_accessed=1_500_000, transcendentals=4096),
    )(place, self_parts, *cross_parts)


PIECES = 4


def add_kernel(kept0_ref, kept1_ref, received0_ref, received1_ref, out_ref, buffer, done):
    wide = COLS // PIECES
    copies = []
    for piece in range(PIECES):
        cols = slice(piece * wide, (piece + 1) * wide)
        kept_ref, received_ref = (
            (kept0_ref, received0_ref) if 2 * piece < PIECES else (kept1_ref, received1_ref)
        )
        inner = slice(cols.start % (COLS // 2), cols.start % (COLS // 2) + wide)
        kept, received = kept_ref[:, inner].astype(F32), received_ref[:, inner].astype(F32)
        buffer[:, cols] = (kept + received).astype(BF16)
        copies.append(
            pltpu.make_async_copy(buffer.at[:, cols], out_ref.at[:, cols], done.at[piece])
        )
        copies[-1].start()
    for copy in copies:
        copy.wait()


def add(kept, received):
    return pl.pallas_call(
        add_kernel,
        out_shape=jax.ShapeDtypeStruct((ROWS, COLS), BF16),
        in_specs=[VMEM] * 4,
        out_specs=pl.BlockSpec(memory_space=pl.ANY),
        scratch_shapes=[pltpu.VMEM((ROWS, COLS), BF16), pltpu.SemaphoreType.DMA((PIECES,))],
        compiler_params=params(),
        name="add",
        cost_estimate=pl.CostEstimate(flops=0, bytes_accessed=1_500_000, transcendentals=0),
    )(*kept, *received)


PIECE = COLS // 2
FETCHES = 8


def fetch_kernel(place_ref, after_ref, w_ref, out_ref, done):
    first = pl.multiple_of(2 * (1 - place_ref[0]) * PIECE, PIECE)
    tall = w_ref.shape[0] // FETCHES
    copies = []
    for part in range(FETCHES):
        rows = slice(part * tall, (part + 1) * tall)
        copies.append(
            pltpu.make_async_copy(
                w_ref.at[rows, pl.ds(first, PIECE)], out_ref.at[rows], done.at[part]
            )
        )
        copies[-1].start()
    for copy in copies:
        copy.wait()


def fetch(place, after, weight):
    anywhere = pl.BlockSpec(memory_space=pl.ANY)
    return pl.pallas_call(
        fetch_kernel,
        out_shape=jax.ShapeDtypeStruct((weight.shape[0], PIECE), weight.dtype),
        in_specs=[SMEM, anywhere, anywhere],
        out_specs=VMEM,
        scratch_shapes=[pltpu.SemaphoreType.DMA((FETCHES,))],
        compiler_params=params(46 * 1024 * 1024),
        name="fetch_weights",
        cost_estimate=pl.CostEstimate(flops=0, bytes_accessed=4_200_000, transcendentals=0),
    )(place, after, weight)


def ring(axis, step):
    count = lax.axis_size(axis)
    return [(i, (i + step) % count) for i in range(count)]


def per_device(queries, keys, values, cross_queries, neighbour_ids, database, out_weight):
    dp = ("xl", "core")
    seq = ("z", "y")
    seq_index = lax.axis_index(seq).astype(jnp.int32).reshape(1)
    y_index = lax.axis_index("y").astype(jnp.int32).reshape(1)
    place_dp = lax.axis_index(dp).astype(jnp.int32).reshape(1)
    across, beside = ring("xl", 1), ring("core", 1)
    up, down = ring("y", 1), ring("y", -1)

    earlier_ids = lax.ppermute(neighbour_ids, seq, [(i, i + 1) for i in range(ZS * YS - 1)])
    own = split_heads(queries[0], keys[0], values[0])
    own, earlier_ids = lax.optimization_barrier((own, earlier_ids))
    own = lax.all_to_all(own, "z", 0, 0, tiled=True)

    mine = cross_queries[0]
    ids = jnp.concatenate([earlier_ids, neighbour_ids], axis=0)
    from_across = lax.ppermute(mine, "xl", across)
    from_beside = lax.ppermute(mine, "core", beside)
    ids_across = lax.ppermute(ids, "xl", across)
    ids_beside = lax.ppermute(ids, "core", beside)
    own_part, beside_part = cross_attend(
        place_dp, (ids, ids_beside), (mine, from_beside), database[0]
    )
    from_across, ids_across, _ = lax.optimization_barrier((from_across, ids_across, own_part))
    from_diagonal = lax.ppermute(from_across, "core", beside)
    ids_diagonal = lax.ppermute(ids_across, "core", beside)
    across_part, diagonal_part = cross_attend(
        place_dp, (ids_across, ids_diagonal), (from_across, from_diagonal), database[0]
    )
    beside_part = lax.ppermute(beside_part, "core", beside)
    diagonal_part = lax.ppermute(diagonal_part, "core", beside)
    own, _, _ = lax.optimization_barrier((own, across_part, beside_part))

    half = ZS // 2
    kv_low, kv_high = own[:half, :2], own[half:, :2]
    below_low = lax.ppermute(kv_low, "y", up)
    above_high = lax.ppermute(kv_high, "y", down)
    below_high = lax.ppermute(kv_high, "y", up)
    above_low = lax.ppermute(kv_low, "y", down)
    across_part = merge(across_part, diagonal_part)
    below_low, above_high, own, _ = lax.optimization_barrier(
        (below_low, above_high, own, across_part)
    )

    far_low = lax.ppermute(below_low, "y", up)
    far_high = lax.ppermute(above_high, "y", down)
    across_part = lax.ppermute(across_part, "xl", across)
    state = attend(y_index, own, (0,), (own,))
    near = (below_low, below_high, above_low, above_high)
    state = attend(y_index, own, (YS - 1, 1), near, state)
    far_low, far_high, state, across_part = lax.optimization_barrier(
        (far_low, far_high, state, across_part)
    )

    self_t = attend(y_index, own, (2,), (far_low, far_high), state, last=True)
    xh = lax.axis_index("xh")
    ready = fetch(xh.astype(jnp.int32).reshape(1), self_t, out_weight)
    self_t = lax.all_to_all(self_t, "z", 0, 0, tiled=True)

    attended = join(seq_index, self_t, (own_part, beside_part, across_part))

    def projected(half):
        columns = lax.dynamic_slice_in_dim(out_weight, half * (COLS // 2), COLS // 2, axis=1)
        return jnp.dot(attended, columns, preferred_element_type=F32).astype(BF16)

    theirs = [jnp.dot(attended, ready, preferred_element_type=F32).astype(BF16)]
    theirs.append(projected(2 * (1 - xh) + 1))
    received = [lax.ppermute(piece, "xh", ring("xh", 1)) for piece in theirs]
    return add([projected(2 * xh + piece) for piece in range(2)], received)[None]


def solution(mesh):
    split = Mesh(mesh.devices.reshape(2, 2, ZS, YS, 2), ("xl", "core", "z", "y", "xh"))
    dp, seq = ("xl", "core"), ("z", "y")
    placed = (
        P(dp, seq, "xh"),
        P(dp, seq, "xh"),
        P(dp, seq, "xh"),
        P(dp, seq, "xh"),
        P(dp, seq, None, None),
        P(dp, None, None, None, "xh"),
        P("xh", None),
    )
    return jax.shard_map(
        per_device, mesh=split, in_specs=placed, out_specs=P(dp, seq, "xh"), check_vma=False
    )
```

```python
import functools
import math

import jax
import jax.numpy as jnp
from jax import lax
from jax.experimental import pallas as pl
from jax.experimental.pallas import tpu as pltpu
from jax.sharding import Mesh, PartitionSpec as P

HD = 128
ROWS = 128
HEADS = 8
ZS, YS = 8, 4
RETR = 128
STAT = 32
LOW = -1e30
EXP2_SCALE = math.log2(math.e) / math.sqrt(HD)
VMEM_LIMIT = 24 * 1024 * 1024

VMEM = pl.BlockSpec(memory_space=pltpu.VMEM)
SMEM = pl.BlockSpec(memory_space=pltpu.SMEM)
F32 = jnp.float32
BF16 = jnp.bfloat16


def params(limit=VMEM_LIMIT):
    return pltpu.CompilerParams(vmem_limit_bytes=limit)


def flipped(block):
    return jnp.transpose(block.astype(F32)).astype(BF16)


def split_kernel(q_ref, k_ref, v_ref, out_ref):
    for h in range(HEADS):
        cols = pl.ds(h * HD, HD)
        out_ref[h, 0] = k_ref[:, cols]
        out_ref[h, 1] = flipped(v_ref[:, cols])
        out_ref[h, 2] = flipped(q_ref[:, cols])


def split_heads(queries, keys, values):
    return pl.pallas_call(
        split_kernel,
        out_shape=jax.ShapeDtypeStruct((HEADS, 3, ROWS, HD), BF16),
        in_specs=[VMEM] * 3,
        out_specs=VMEM,
        compiler_params=params(56 * 1024 * 1024),
        name="split_heads",
        cost_estimate=pl.CostEstimate(flops=0, bytes_accessed=1536 * 1024, transcendentals=0),
    )(queries, keys, values)


def shade_of(y, step):
    return jnp.where(lax.rem(y + step, YS) < y, 0.0, LOW).astype(F32)


def fold(state, scores, v_tile):
    row_max, total, summed = state
    new_max = jnp.maximum(row_max, jnp.max(scores, axis=0, keepdims=True))
    weights = jnp.exp2((scores - new_max) * EXP2_SCALE)
    fade = jnp.exp2((row_max - new_max) * EXP2_SCALE)
    total = total * fade + jnp.sum(weights, axis=0, keepdims=True)
    summed = summed * fade + jnp.dot(v_tile, weights.astype(BF16), preferred_element_type=F32)
    return new_max, total, summed


def attend_kernel(steps, count, first, last, y_ref, own_ref, *refs):
    part_refs, refs = refs[:count], refs[count:]
    if not first:
        old_refs, refs = refs[:3], refs[3:]
    wide, results = refs[-1], refs[:-1]
    y = y_ref[0]
    left = lax.broadcasted_iota(jnp.int32, (1, 2 * ROWS), 1) < ROWS
    key_pos = lax.broadcasted_iota(jnp.int32, (ROWS, 2 * ROWS), 0)
    query_pos = lax.broadcasted_iota(jnp.int32, (ROWS, 2 * ROWS), 1)
    halves = count // len(steps)

    def block(part, z, kind):
        depth = ZS // halves
        return part_refs[part * halves + z // depth][z % depth, kind]

    for pair in range(ZS // 2):
        low, high = 2 * pair, 2 * pair + 1
        wide[:, 0:ROWS] = own_ref[low, 2]
        wide[:, ROWS:] = own_ref[high, 2]
        places = [(part, z) for part in range(len(steps)) for z in range(high + 1)]
        k_tile = jnp.concatenate([block(part, z, 0) for part, z in places], axis=0)
        v_tile = jnp.concatenate([block(part, z, 1) for part, z in places], axis=1)
        scores = jnp.dot(k_tile, wide[...], preferred_element_type=F32)
        pieces = []
        for part, step in enumerate(steps):
            start = part * (high + 1) * ROWS
            middle, end = start + low * ROWS, start + high * ROWS
            if step == 0:
                same_z = jnp.where(left & (key_pos > query_pos), LOW, 0.0)
                next_z = jnp.where(left | (key_pos > query_pos - ROWS), LOW, 0.0)
            else:
                shade = shade_of(y, step)
                same_z, next_z = jnp.where(left, shade, 0.0), jnp.where(left, LOW, shade)
            if low:
                pieces.append(scores[start:middle])
            pieces.append(scores[middle:end] + same_z)
            pieces.append(scores[end : end + ROWS] + next_z)
        scores = jnp.concatenate(pieces, axis=0)
        if first:
            row_max = jnp.max(scores, axis=0, keepdims=True)
            weights = jnp.exp2((scores - row_max) * EXP2_SCALE)
            total = jnp.sum(weights, axis=0, keepdims=True)
            summed = jnp.dot(v_tile, weights.astype(BF16), preferred_element_type=F32)
        else:
            old = [
                jnp.concatenate([ref[z : z + 1, :] for z in (low, high)], axis=1)
                for ref in old_refs[:2]
            ] + [jnp.concatenate([old_refs[2][z] for z in (low, high)], axis=1)]
            row_max, total, summed = fold(old, scores, v_tile)
        for z, side in ((low, slice(0, ROWS)), (high, slice(ROWS, None))):
            if last:
                results[0][z] = (summed[:, side] * (1.0 / total[:, side])).astype(BF16)
            else:
                results[0][z : z + 1, :] = row_max[:, side]
                results[1][z : z + 1, :] = total[:, side]
                results[2][z] = summed[:, side]


def attend(y_index, own, steps, parts, state=(), last=False):
    rows = jax.ShapeDtypeStruct((ZS, ROWS), F32)
    kept = (rows, rows, jax.ShapeDtypeStruct((ZS, HD, ROWS), F32))
    share = len(steps)
    return pl.pallas_call(
        functools.partial(attend_kernel, steps, len(parts), not state, last),
        out_shape=jax.ShapeDtypeStruct((ZS, HD, ROWS), BF16) if last else kept,
        in_specs=[SMEM] + [VMEM] * (1 + len(parts) + len(state)),
        out_specs=VMEM if last else (VMEM,) * 3,
        scratch_shapes=[pltpu.VMEM((HD, 2 * ROWS), BF16)],
        compiler_params=params(),
        name="attend_far" if last else "attend_near",
        cost_estimate=pl.CostEstimate(
            flops=350_000_000 * share, bytes_accessed=1_500_000, transcendentals=650_000 * share
        ),
    )(y_index, own, *parts, *state)


def cross_kernel(ids0_ref, ids1_ref, place_ref, q0_ref, q1_ref, db_ref, out0_ref, out1_ref, *refs):
    top, total, summed, blocks, ready = refs
    here = place_ref[0]

    def named(ids_ref, index):
        which, span, n = (index + 2) // 4, lax.rem(index // 2 + 1, 2), lax.rem(index, 2)
        return ids_ref[which, span, n, 0], ids_ref[which, span, n, 1]

    def fetch_block(block, place):
        return pltpu.make_async_copy(db_ref.at[:, block], blocks.at[place], ready.at[place])

    for slot, ids_ref in enumerate((ids0_ref, ids1_ref)):

        def request(index, carry, slot=slot, ids_ref=ids_ref):
            shard, block = named(ids_ref, index)

            @pl.when(shard == here)
            def _():
                fetch_block(block, 6 * slot + index).start()

            return carry

        lax.fori_loop(0, 6, request, 0)
    row = lax.broadcasted_iota(jnp.int32, (1, ROWS), 1)
    group_of = (row + 1) // 64
    for slot, ids_ref, q_ref, out_ref in (
        (0, ids0_ref, q0_ref, out0_ref),
        (1, ids1_ref, q1_ref, out1_ref),
    ):
        top[...] = jnp.full(top.shape, LOW, F32)
        total[...] = jnp.zeros(total.shape, F32)
        summed[...] = jnp.zeros(summed.shape, F32)

        def neighbour(index, carry, slot=slot, ids_ref=ids_ref, q_ref=q_ref):
            shard, block = named(ids_ref, index)
            place = 6 * slot + index

            @pl.when(shard == here)
            def _():
                fetch_block(block, place).wait()
                inside = group_of == index // 2
                cols = [slice(h * HD, (h + 1) * HD) for h in range(HEADS)]
                scores = [
                    lax.dot_general(
                        blocks[place, 0, :, c],
                        q_ref[:, c],
                        (((1,), (1,)), ((), ())),
                        preferred_element_type=F32,
                    )
                    for c in cols
                ]
                old_max = top[...]
                new_max = jnp.concatenate(
                    [jnp.max(block_scores, axis=0, keepdims=True) for block_scores in scores], axis=0
                )
                new_max = jnp.where(inside, jnp.maximum(old_max, new_max), old_max)
                fade = jnp.exp2((old_max - new_max) * EXP2_SCALE)
                weights = [
                    jnp.where(
                        inside, jnp.exp2((scores[h] - new_max[h : h + 1]) * EXP2_SCALE), 0.0
                    )
                    for h in range(HEADS)
                ]
                sums = [jnp.sum(w, axis=0, keepdims=True) for w in weights]
                products = [
                    lax.dot_general(
                        blocks[place, 1, :, cols[h]],
                        weights[h].astype(BF16),
                        (((0,), (0,)), ((), ())),
                        preferred_element_type=F32,
                    )
                    for h in range(HEADS)
                ]
                top[...] = new_max
                total[...] = total[...] * fade + jnp.concatenate(sums, axis=0)
                for h in range(HEADS):
                    summed[h] = summed[h] * fade[h : h + 1] + products[h]

            return carry

        lax.fori_loop(0, 6, neighbour, 0)
        sums = total[...]
        some = sums > 0.0
        safe = jnp.where(some, sums, 1.0)
        inverse = 1.0 / safe
        for h in range(HEADS):
            out_ref[h * HD : (h + 1) * HD, :] = (summed[h] * inverse[h : h + 1, :]).astype(BF16)
        level = jnp.where(some, top[...] * EXP2_SCALE + jnp.log2(safe), LOW)
        store_level(out_ref, level)


def cross_attend(place, ids, queries, database):
    shape = jax.ShapeDtypeStruct((HEADS * HD + STAT, ROWS), BF16)
    return pl.pallas_call(
        cross_kernel,
        out_shape=(shape,) * 2,
        in_specs=[SMEM] * 3 + [VMEM] * 2 + [pl.BlockSpec(memory_space=pl.ANY)],
        out_specs=(VMEM,) * 2,
        scratch_shapes=[
            pltpu.VMEM((HEADS, ROWS), F32),
            pltpu.VMEM((HEADS, ROWS), F32),
            pltpu.VMEM((HEADS, HD, ROWS), F32),
            pltpu.VMEM((12, 2, RETR, HEADS * HD), BF16),
            pltpu.SemaphoreType.DMA((12,)),
        ],
        compiler_params=params(52 * 1024 * 1024),
        name="cross_attend",
        cost_estimate=pl.CostEstimate(
            flops=2_000_000_000, bytes_accessed=5_000_000, transcendentals=1_000_000
        ),
    )(*ids, place, *queries, database)


def level_of(part_ref):
    stats = part_ref[HEADS * HD :, :].astype(F32)
    return stats[0:8] + stats[8:16] + stats[16:24]


def store_level(out_ref, level):
    high = level.astype(BF16).astype(F32)
    middle = (level - high).astype(BF16).astype(F32)
    low = level - high - middle
    stats = jnp.concatenate([high, middle, low, jnp.zeros_like(low)], axis=0)
    out_ref[HEADS * HD :, :] = stats.astype(BF16)


def merge_kernel(first_ref, second_ref, out_ref):
    levels = [level_of(first_ref), level_of(second_ref)]
    top = jnp.maximum(*levels)
    shares = [jnp.exp2(level - top) for level in levels]
    whole = shares[0] + shares[1]
    shares = [share / whole for share in shares]
    for h in range(HEADS):
        cols = slice(h * HD, (h + 1) * HD)
        first = first_ref[cols, :].astype(F32) * shares[0][h : h + 1, :]
        second = second_ref[cols, :].astype(F32) * shares[1][h : h + 1, :]
        out_ref[cols, :] = (first + second).astype(BF16)
    store_level(out_ref, top + jnp.log2(whole))


def merge(first, second):
    return pl.pallas_call(
        merge_kernel,
        out_shape=jax.ShapeDtypeStruct(first.shape, BF16),
        in_specs=[VMEM] * 2,
        out_specs=VMEM,
        compiler_params=params(),
        name="merge",
        cost_estimate=pl.CostEstimate(flops=0, bytes_accessed=800_000, transcendentals=4096),
    )(first, second)


COLS = 2048


def join_kernel(place_ref, self_ref, *refs):
    part_refs, att_ref = refs[0:3], refs[3]
    row = lax.broadcasted_iota(jnp.int32, (1, ROWS), 1)
    live = jnp.where((row >= 63) | (place_ref[0] > 0), 1.0, 0.0).astype(F32)
    levels = [level_of(part) for part in part_refs]
    top = functools.reduce(jnp.maximum, levels)
    shares = [jnp.exp2(level - top) for level in levels]
    whole = functools.reduce(jnp.add, shares)
    shares = [share / whole * live for share in shares]
    for h in range(HEADS):
        cols = slice(h * HD, (h + 1) * HD)
        joined = self_ref[h].astype(F32)
        for part, share in zip(part_refs, shares):
            joined = joined + part[cols, :].astype(F32) * share[h : h + 1, :]
        att_ref[:, cols] = jnp.transpose(joined).astype(BF16)


def join(place, self_parts, cross_parts):
    return pl.pallas_call(
        join_kernel,
        out_shape=jax.ShapeDtypeStruct((ROWS, HEADS * HD), BF16),
        in_specs=[SMEM] + [VMEM] * 4,
        out_specs=VMEM,
        compiler_params=params(),
        name="join",
        cost_estimate=pl.CostEstimate(flops=0, bytes_accessed=1_500_000, transcendentals=4096),
    )(place, self_parts, *cross_parts)


PIECES = 4


def add_kernel(kept0_ref, kept1_ref, received0_ref, received1_ref, out_ref, buffer, done):
    wide = COLS // PIECES
    copies = []
    for piece in range(PIECES):
        cols = slice(piece * wide, (piece + 1) * wide)
        kept_ref, received_ref = (
            (kept0_ref, received0_ref) if 2 * piece < PIECES else (kept1_ref, received1_ref)
        )
        inner = slice(cols.start % (COLS // 2), cols.start % (COLS // 2) + wide)
        kept, received = kept_ref[:, inner].astype(F32), received_ref[:, inner].astype(F32)
        buffer[:, cols] = (kept + received).astype(BF16)
        copies.append(
            pltpu.make_async_copy(buffer.at[:, cols], out_ref.at[:, cols], done.at[piece])
        )
        copies[-1].start()
    for copy in copies:
        copy.wait()


def add(kept, received):
    return pl.pallas_call(
        add_kernel,
        out_shape=jax.ShapeDtypeStruct((ROWS, COLS), BF16),
        in_specs=[VMEM] * 4,
        out_specs=pl.BlockSpec(memory_space=pl.ANY),
        scratch_shapes=[pltpu.VMEM((ROWS, COLS), BF16), pltpu.SemaphoreType.DMA((PIECES,))],
        compiler_params=params(),
        name="add",
        cost_estimate=pl.CostEstimate(flops=0, bytes_accessed=1_500_000, transcendentals=0),
    )(*kept, *received)


PIECE = COLS // 2
FETCHES = 8


def fetch_kernel(place_ref, after_ref, w_ref, out_ref, done):
    first = pl.multiple_of(2 * (1 - place_ref[0]) * PIECE, PIECE)
    tall = w_ref.shape[0] // FETCHES
    copies = []
    for part in range(FETCHES):
        rows = slice(part * tall, (part + 1) * tall)
        copies.append(
            pltpu.make_async_copy(
                w_ref.at[rows, pl.ds(first, PIECE)], out_ref.at[rows], done.at[part]
            )
        )
        copies[-1].start()
    for copy in copies:
        copy.wait()


def fetch(place, after, weight):
    anywhere = pl.BlockSpec(memory_space=pl.ANY)
    return pl.pallas_call(
        fetch_kernel,
        out_shape=jax.ShapeDtypeStruct((weight.shape[0], PIECE), weight.dtype),
        in_specs=[SMEM, anywhere, anywhere],
        out_specs=VMEM,
        scratch_shapes=[pltpu.SemaphoreType.DMA((FETCHES,))],
        compiler_params=params(46 * 1024 * 1024),
        name="fetch_weights",
        cost_estimate=pl.CostEstimate(flops=0, bytes_accessed=4_200_000, transcendentals=0),
    )(place, after, weight)


def ring(axis, step):
    count = lax.axis_size(axis)
    return [(i, (i + step) % count) for i in range(count)]


def per_device(queries, keys, values, cross_queries, neighbour_ids, database, out_weight):
    dp = ("xl", "core")
    seq = ("z", "y")
    seq_index = lax.axis_index(seq).astype(jnp.int32).reshape(1)
    y_index = lax.axis_index("y").astype(jnp.int32).reshape(1)
    place_dp = lax.axis_index(dp).astype(jnp.int32).reshape(1)
    across, beside = ring("xl", 1), ring("core", 1)
    up, down = ring("y", 1), ring("y", -1)

    earlier_ids = lax.ppermute(neighbour_ids, seq, [(i, i + 1) for i in range(ZS * YS - 1)])
    own = split_heads(queries[0], keys[0], values[0])
    own, earlier_ids = lax.optimization_barrier((own, earlier_ids))
    own = lax.all_to_all(own, "z", 0, 0, tiled=True)

    mine = cross_queries[0]
    ids = jnp.concatenate([earlier_ids, neighbour_ids], axis=0)
    from_across = lax.ppermute(mine, "xl", across)
    from_beside = lax.ppermute(mine, "core", beside)
    ids_across = lax.ppermute(ids, "xl", across)
    ids_beside = lax.ppermute(ids, "core", beside)
    ids_diagonal = lax.ppermute(ids, dp, [(i, 3 - i) for i in range(4)])
    own_part, beside_part = cross_attend(
        place_dp, (ids, ids_beside), (mine, from_beside), database[0]
    )
    from_across, ids_across, ids_diagonal, _ = lax.optimization_barrier(
        (from_across, ids_across, ids_diagonal, own_part)
    )
    from_diagonal = lax.ppermute(from_across, "core", beside)
    across_part, diagonal_part = cross_attend(
        place_dp, (ids_across, ids_diagonal), (from_across, from_diagonal), database[0]
    )
    beside_part = lax.ppermute(beside_part, "core", beside)
    diagonal_part = lax.ppermute(diagonal_part, "core", beside)
    own, _, _ = lax.optimization_barrier((own, across_part, beside_part))

    half = ZS // 2
    kv_low, kv_high = own[:half, :2], own[half:, :2]
    below_low = lax.ppermute(kv_low, "y", up)
    above_high = lax.ppermute(kv_high, "y", down)
    below_high = lax.ppermute(kv_high, "y", up)
    above_low = lax.ppermute(kv_low, "y", down)
    across_part = merge(across_part, diagonal_part)
    below_low, above_high, own, _ = lax.optimization_barrier(
        (below_low, above_high, own, across_part)
    )

    far_low = lax.ppermute(below_low, "y", up)
    far_high = lax.ppermute(above_high, "y", down)
    across_part = lax.ppermute(across_part, "xl", across)
    state = attend(y_index, own, (0,), (own,))
    near = (below_low, below_high, above_low, above_high)
    state = attend(y_index, own, (YS - 1, 1), near, state)
    far_low, far_high, state, across_part = lax.optimization_barrier(
        (far_low, far_high, state, across_part)
    )

    self_t = attend(y_index, own, (2,), (far_low, far_high), state, last=True)
    xh = lax.axis_index("xh")
    ready = fetch(xh.astype(jnp.int32).reshape(1), self_t, out_weight)
    self_t = lax.all_to_all(self_t, "z", 0, 0, tiled=True)

    attended = join(seq_index, self_t, (own_part, beside_part, across_part))

    def projected(half):
        columns = lax.dynamic_slice_in_dim(out_weight, half * (COLS // 2), COLS // 2, axis=1)
        return jnp.dot(attended, columns, preferred_element_type=F32).astype(BF16)

    theirs = [jnp.dot(attended, ready, preferred_element_type=F32).astype(BF16)]
    theirs.append(projected(2 * (1 - xh) + 1))
    received = [lax.ppermute(piece, "xh", ring("xh", 1)) for piece in theirs]
    return add([projected(2 * xh + piece) for piece in range(2)], received)[None]


def solution(mesh):
    split = Mesh(mesh.devices.reshape(2, 2, ZS, YS, 2), ("xl", "core", "z", "y", "xh"))
    dp, seq = ("xl", "core"), ("z", "y")
    placed = (
        P(dp, seq, "xh"),
        P(dp, seq, "xh"),
        P(dp, seq, "xh"),
        P(dp, seq, "xh"),
        P(dp, seq, None, None),
        P(dp, None, None, None, "xh"),
        P("xh", None),
    )
    return jax.shard_map(
        per_device, mesh=split, in_specs=placed, out_specs=P(dp, seq, "xh"), check_vma=False
    )
```
